128 devices in a mesh: seq: 16 (over z, y), tp: 8 (over x, core).
Axes of the slice: x: 4, y: 4, z: 4, core: 2. Of those that a mesh axis runs over, the one named last changes fastest.
Arguments:
- normed: bfloat16 [4, 16384, 1024], P(None, 'seq'), may hold values from -6 to 6
- grad_out: bfloat16 [4, 16384, 1024], P(None, 'seq'), may hold values from -16 to 16
- value_weight: bfloat16 [1024, 1024], P(None, 'tp'), may hold values from -0.1875 to 0.1875
- gate_weight: bfloat16 [1024, 1024], P(None, 'tp'), may hold values from -0.1875 to 0.1875
- depth_taps: float32 [9, 1024], P(None, 'tp'), may hold values from -2 to 2
- norm_gain: float32 [1024], P('tp'), may hold values from 0.1 to 1.9
- norm_shift: float32 [1024], P('tp'), may hold values from -1 to 1
- out_weight: bfloat16 [1024, 1024], P(None, 'tp'), may hold values from -0.1875 to 0.1875
- lengths: int32 [4], replicated, may hold values from 4096 to 16384, as said below
Outputs:
- grad_in: bfloat16 [4, 1024, 16384], P(None, ('seq', 'tp'))
- grad_w_value: float32 [1024, 1024], P('seq', 'tp')
- grad_w_gate: float32 [1024, 1024], P('seq', 'tp')
- grad_w_out: float32 [1024, 1024], P('seq', 'tp')
- grad_taps: float32 [9, 1024], P(None, 'tp')
- grad_gain: float32 [1024], P('tp')
- grad_shift: float32 [1024], P('tp')
The draws below stay inside these ranges and needn't reach their ends.
Inputs may be any that keep to these rules, and one draw needn't show every extreme that they name: `lengths`: frames of each recording that are valid; some recording is valid to its last frame.
All inputs are finite; a program needn't handle non-finite values.
Results may differ from the reference program's by a relative error of at most 0.01.
Values may be sent and summed in bfloat16 or wider, within the bound.
A program may use at most 128 MiB of HBM per device.

```python
import math
import jax
import jax.numpy as jnp
from jax import lax

D = 1024
C = 1024
KERNEL = 9
RECS = 4
L = 16384
N_TP = 8


def draw_grad_out(key, part):
    first, second = jax.random.split(jax.random.fold_in(key, 11), 2)
    base = jnp.clip(jax.random.normal(first, (RECS, L, D), jnp.float32), -6.0, 6.0)
    log_scale = jax.random.uniform(second, (RECS, L, 1), jnp.float32, 0.0, math.log(10.0))
    values = 0.1 * base * jnp.exp(log_scale)
    return jnp.clip(values, -16.0, 16.0).astype(jnp.bfloat16)


def draw_lengths(key, part):
    first, second = jax.random.split(jax.random.fold_in(key, 5))
    drawn = jax.random.randint(first, (RECS,), L // 4, L + 1)
    whole_one = jax.random.randint(second, (), 0, RECS)
    return jnp.where(jnp.arange(RECS) == whole_one, L, drawn).astype(jnp.int32)


def steps_of(own_key, extent, shards, least, top_value):
    level, own = 1.0, jax.random.fold_in(own_key, 6)
    for position, parts in shards:
        draws = jnp.exp(jax.random.uniform(jax.random.fold_in(own, position), (parts,), jnp.float32, least / len(shards), top_value / len(shards)))
        level = level * jnp.repeat(draws, extent[position] // parts).reshape([-1 if axis == position else 1 for axis in range(len(extent))])
    return level


def normal_values(key, shape, deviation, limit, pieces=(), held_as=jnp.bfloat16):
    loudness = steps_of(key, shape, pieces, -0.22, 0.18) if pieces else 1.0
    result = jax.random.normal(key, shape, jnp.float32) * deviation * loudness
    return jnp.minimum(jnp.maximum(result, -limit), limit).astype(held_as)


def setup_inputs(seed: int = 0) -> dict:
    key_list = jax.random.split(jax.random.key(seed), 10)
    return {
        "normed": normal_values(key_list[0], (RECS, L, D), 1.0, 6.0, ((1, 16),)),
        "grad_out": draw_grad_out(jax.random.fold_in(key_list[9], 71), 0),
        "value_weight": normal_values(key_list[2], (D, C), D ** -0.5, 0.1875, ((1, 8),)),
        "gate_weight": normal_values(key_list[3], (D, C), D ** -0.5, 0.1875, ((1, 8),)),
        "depth_taps": normal_values(key_list[4], (KERNEL, C), KERNEL ** -0.5, 2.0, ((1, 8),), jnp.float32),
        "norm_gain": jnp.clip(1.0 + 0.18 * jax.random.normal(key_list[5], (C,), jnp.float32), 0.1, 1.9),
        "norm_shift": jnp.clip(jax.random.uniform(key_list[6], (C,), jnp.float32, -1.0, 1.0) * steps_of(key_list[6], (C,), ((0, 8),), -0.4, 0.0), -1.0, 1.0),
        "out_weight": normal_values(key_list[7], (D, C), C ** -0.5, 0.1875, ((1, 8),)),
        "lengths": draw_lengths(jax.random.fold_in(key_list[9], 71), 0),
    }


epsilon = 1e-05

def reference(normed, grad_out, value_weight, gate_weight, depth_taps, norm_gain, norm_shift, out_weight, lengths):
    frames_all = RECS * L
    margin = (KERNEL - 1) // 2
    positions = jnp.arange(L, dtype=jnp.int32)
    valid_mask = (positions[None, :] < lengths[:, None]).astype(jnp.float32)[:, :, None]
    frame_count = jnp.sum(lengths).astype(jnp.float32)
    rows_in = normed.reshape(frames_all, D)
    value_lin = jnp.dot(rows_in, value_weight, preferred_element_type=jnp.float32).reshape(RECS, L, C)
    gate_lin = jnp.dot(rows_in, gate_weight, preferred_element_type=jnp.float32).reshape(RECS, L, C)
    gate_sig = jax.nn.sigmoid(gate_lin)
    gated_units = valid_mask * value_lin * gate_sig
    gated_pad = jnp.pad(gated_units, ((0, 0), (margin, margin), (0, 0)))
    conv_out = jnp.zeros((RECS, L, C), jnp.float32)
    for tap_index in range(KERNEL):
        conv_out = conv_out + depth_taps[tap_index] * gated_pad[:, tap_index:tap_index + L]
    channel_sum = lax.optimization_barrier(jnp.sum(valid_mask * conv_out, axis=(0, 1)))
    channel_sq = lax.optimization_barrier(jnp.sum(valid_mask * conv_out * conv_out, axis=(0, 1)))
    centre = channel_sum / frame_count
    spread = channel_sq / frame_count - centre * centre
    inv_std = lax.rsqrt(spread + epsilon)
    unit_conv = (conv_out - centre) * inv_std
    normalized = unit_conv * norm_gain + norm_shift
    norm_sig = jax.nn.sigmoid(normalized)
    swished = (valid_mask * normalized * norm_sig).astype(jnp.bfloat16)
    grads_flat = grad_out.reshape(frames_all, D)
    swish_grad = jnp.dot(grads_flat, out_weight, preferred_element_type=jnp.float32).reshape(RECS, L, C)
    grad_w_out = lax.dot_general(grads_flat, swished.reshape(frames_all, C), (((0,), (0,)), ((), ())), preferred_element_type=jnp.float32)
    grad_norm = swish_grad * valid_mask * norm_sig * (1.0 + normalized * (1.0 - norm_sig))
    grad_shift = lax.optimization_barrier(jnp.sum(grad_norm, axis=(0, 1)))
    grad_gain = lax.optimization_barrier(jnp.sum(grad_norm * unit_conv, axis=(0, 1)))
    grad_conv = valid_mask * norm_gain * inv_std * (grad_norm - grad_shift / frame_count - unit_conv * grad_gain / frame_count)
    tap_list = []
    for tap_index in range(KERNEL):
        tap_list.append(lax.optimization_barrier(jnp.sum(grad_conv * gated_pad[:, tap_index:tap_index + L], axis=(0, 1))))
    grad_taps = jnp.stack(tap_list)
    conv_pad = jnp.pad(grad_conv, ((0, 0), (margin, margin), (0, 0)))
    grad_gated = jnp.zeros((RECS, L, C), jnp.float32)
    for tap_index in range(KERNEL):
        first_row = 2 * margin - tap_index
        grad_gated = grad_gated + depth_taps[tap_index] * conv_pad[:, first_row:first_row + L]
    grad_gated = valid_mask * grad_gated
    grad_value = (grad_gated * gate_sig).astype(jnp.bfloat16).reshape(frames_all, C)
    grad_gate = (grad_gated * value_lin * gate_sig * (1.0 - gate_sig)).astype(jnp.bfloat16).reshape(frames_all, C)
    grad_w_value = lax.dot_general(rows_in, grad_value, (((0,), (0,)), ((), ())), preferred_element_type=jnp.float32)
    grad_w_gate = lax.dot_general(rows_in, grad_gate, (((0,), (0,)), ((), ())), preferred_element_type=jnp.float32)
    group_width = C // N_TP

    def add_group(running, group_index):
        first_col = (group_index * group_width).astype(jnp.int32)
        value_part = lax.dynamic_slice_in_dim(grad_value, first_col, group_width, 1)
        gate_part = lax.dynamic_slice_in_dim(grad_gate, first_col, group_width, 1)
        value_cols = lax.dynamic_slice_in_dim(value_weight, first_col, group_width, 1)
        gate_cols = lax.dynamic_slice_in_dim(gate_weight, first_col, group_width, 1)
        partial_value = lax.dot_general(value_part, value_cols, (((1,), (1,)), ((), ())), preferred_element_type=jnp.float32)
        partial_value = partial_value + lax.dot_general(gate_part, gate_cols, (((1,), (1,)), ((), ())), preferred_element_type=jnp.float32)
        rounded = lax.optimization_barrier(partial_value.astype(jnp.bfloat16))
        return (running + rounded.astype(jnp.float32), None)
    groups = jnp.arange(N_TP, dtype=jnp.int32)
    grad_normed, _ = lax.scan(add_group, jnp.zeros((frames_all, D), jnp.float32), groups)
    grad_rows = (grads_flat.astype(jnp.float32) + grad_normed).astype(jnp.bfloat16).reshape(RECS, L, D)
    grad_in = jnp.transpose(grad_rows, (0, 2, 1))
    return (grad_in, grad_w_value, grad_w_gate, grad_w_out, grad_taps, grad_gain, grad_shift)
```

```python
import functools

import jax
import jax.numpy as jnp
from jax import lax
from jax.experimental import pallas as pl
from jax.experimental.pallas import tpu as pltpu
from jax.sharding import PartitionSpec as P

MESH = pl.DeviceIdType.MESH
F32 = jnp.float32
BF16 = jnp.bfloat16
EPS = 1e-05
LANES = 128
EDGE = 8
XN = 4


def mm(a, b):
    return jnp.dot(a, b, preferred_element_type=F32)


def mm_t(a, b):
    return lax.dot_general(a, b, (((1,), (1,)), ((), ())), preferred_element_type=F32)


def mm_tl(a, b):
    return lax.dot_general(a, b, (((0,), (0,)), ((), ())), preferred_element_type=F32)


def fold(v):
    rows = v.shape[0]
    return jnp.sum(v.reshape(rows // 8, 8, LANES), axis=0)


def kernel(
    cfg,
    lengths,
    normed_h,
    grads_h,
    wv_h,
    wg_h,
    wo_h,
    taps,
    gain,
    shift,
    gin,
    gwv,
    gwg,
    gwo,
    gtaps,
    ggain,
    gshift,
    nv,
    gv,
    wcat,
    wo,
    wd_own,
    wd_send,
    wd_oth,
    gp,
    gs,
    a2,
    cv,
    gn,
    gc,
    sw,
    halo,
    red_a,
    red_b,
    red_c,
    got,
    gbuf,
    goth,
    s2,
    r2,
    sx,
    rx,
    osend,
    tacc,
    wacc,
    woacc,
    wsend,
    wrecv,
    load_sem,
    halo_send,
    halo_recv,
    red_send,
    red_recv,
    wx_send,
    wx_recv,
    ge_send,
    ge_recv,
    d2_send,
    d2_recv,
    nb_send,
    nb_recv,
    aa_send,
    aa_recv,
    aa_own,
    wr_send,
    wr_recv,
):
    R, NF, D, NS, F, TM, TC = cfg
    K = taps.shape[0]
    H = (K - 1) // 2
    M = 8 * NS
    NCH = R * NF // F
    cpr = NF // F
    HF = F // 2
    DP = D // NS
    s = lax.axis_index("seq")
    t = lax.axis_index("tp")
    x = lax.div(t, 2)
    core = lax.rem(t, 2)
    other = x * 2 + (1 - core)
    right = lax.rem(x + 1, XN) * 2 + core
    left = lax.rem(x + XN - 1, XN) * 2 + core
    up = lax.rem(s + 1, NS)
    down = lax.rem(s + NS - 1, NS)

    barrier = pltpu.get_barrier_semaphore()

    def greet(k, carry):
        pl.semaphore_signal(
            barrier, inc=1, device_id=(lax.rem(s + k, NS), t), device_id_type=MESH
        )
        return carry

    lax.fori_loop(1, NS, greet, 0)
    for mate in (other, right, left):
        pl.semaphore_signal(barrier, inc=1, device_id=(s, mate), device_id_type=MESH)

    loads = [
        pltpu.make_async_copy(wv_h, wcat.at[:, 0:LANES], load_sem.at[0]),
        pltpu.make_async_copy(wg_h, wcat.at[:, LANES : 2 * LANES], load_sem.at[1]),
        pltpu.make_async_copy(wo_h, wo, load_sem.at[2]),
    ]
    for load in loads:
        load.start()

    def normed_load(r):
        return pltpu.make_async_copy(normed_h.at[r], nv.at[r], load_sem.at[3 + r])

    def grads_load(r):
        return pltpu.make_async_copy(grads_h.at[r], gv.at[r], load_sem.at[3 + R + r])

    for r in range(R):
        normed_load(r).start()
    for r in range(R):
        grads_load(r).start()

    def valid(r, row0, rows):
        at = s * NF + row0 + lax.broadcasted_iota(jnp.int32, (rows, LANES), 0)
        return jnp.logical_and(at >= 0, at < lengths[r])

    def picker(xd, cd):
        row = lax.broadcasted_iota(jnp.int32, (M, D), 0)
        col = lax.broadcasted_iota(jnp.int32, (M, D), 1)
        want = (row // 8) * 64 + xd * 16 + cd * 8 + row % 8
        return jnp.where(col == want, 1.0, 0.0).astype(BF16)

    loads[0].wait()
    loads[1].wait()

    def pick_weights(xd, carry):
        rows = pl.ds(pl.multiple_of(xd * M, M), M)
        wd_own[rows, :] = mm(picker(xd, core), wcat[...]).astype(BF16)
        wd_send[rows, :] = mm(picker(xd, 1 - core), wcat[...]).astype(BF16)
        return carry

    lax.fori_loop(0, XN, pick_weights, 0)
    tacc[...] = jnp.zeros_like(tacc)
    wacc[...] = jnp.zeros_like(wacc)
    woacc[...] = jnp.zeros_like(woacc)

    pl.semaphore_wait(barrier, NS - 1 + 3)

    def remote(src, dst, send, recv, device):
        return pltpu.make_async_remote_copy(
            src_ref=src,
            dst_ref=dst,
            send_sem=send,
            recv_sem=recv,
            device_id=device,
            device_id_type=MESH,
        )

    weight_swap = remote(wd_send, wd_oth, wx_send, wx_recv, (s, other))
    weight_swap.start()

    def edge_copies(kind, field, r):
        index = kind * 2 * R + 2 * r
        return (
            remote(
                field.at[r, pl.ds(NF, EDGE)],
                halo.at[kind, r, 0],
                halo_send.at[index],
                halo_recv.at[index],
                (up, t),
            ),
            remote(
                field.at[r, pl.ds(EDGE, EDGE)],
                halo.at[kind, r, 1],
                halo_send.at[index + 1],
                halo_recv.at[index + 1],
                (down, t),
            ),
        )

    def send_edges(kind, field, r):
        for copy in edge_copies(kind, field, r):
            copy.start()

    def take_edges(kind, field, r):
        low, high = edge_copies(kind, field, r)
        low.wait_recv()
        high.wait_recv()
        field[r, 0:EDGE] = jnp.where(s > 0, halo[kind, r, 0], 0.0)
        field[r, NF + EDGE : NF + 2 * EDGE] = jnp.where(s < NS - 1, halo[kind, r, 1], 0.0)

    per_rec = NF // TM

    def forward(i, carry):
        r = lax.div(i, per_rec)
        part = lax.rem(i, per_rec)
        row0 = pl.multiple_of(part * TM, TM)
        rows = pl.ds(row0, TM)

        @pl.when(part == 0)
        def _():
            normed_load(r).wait()

        both = mm(nv[r, rows, :], wcat[...])
        gate = jax.nn.sigmoid(both[:, LANES:])
        unit = both[:, :LANES] * gate
        gp[r, pl.ds(row0 + EDGE, TM)] = jnp.where(valid(r, row0, TM), unit, 0.0)
        gs[r, rows] = gate
        a2[r, rows] = unit * (1.0 - gate)

        @pl.when(part == per_rec - 1)
        def _():
            send_edges(0, gp, r)

        return carry

    lax.fori_loop(0, R * per_rec, forward, 0)

    tap_rows = [taps[k : k + 1, :] for k in range(K)]
    tiles = NF // TC
    zero = jnp.zeros((8, LANES), F32)

    def conv_rec(r, sums):
        take_edges(0, gp, r)

        def conv_tile(i, sums):
            row0 = pl.multiple_of(i * TC, TC)
            total = tap_rows[0] * gp[r, pl.ds(row0 + EDGE - H, TC)]
            for k in range(1, K):
                total = total + tap_rows[k] * gp[r, pl.ds(row0 + EDGE - H + k, TC)]
            cv[r, pl.ds(row0 + EDGE, TC)] = total
            kept = jnp.where(valid(r, row0, TC), total, 0.0)
            return sums[0] + fold(kept), sums[1] + fold(kept * kept)

        sums = lax.fori_loop(0, tiles, conv_tile, sums)
        send_edges(1, cv, r)
        return sums

    sums = lax.fori_loop(0, R, conv_rec, (zero, zero))

    def red_wait(red, index):
        part = red.at[pl.ds(0, NS - 1)]
        pltpu.make_async_copy(part, part, red_recv.at[index]).wait()

    def red_sent(red, index):
        part = red.at[pl.ds(0, NS - 1)]
        pltpu.make_async_copy(part, part, red_send.at[index]).wait()

    def spread(red, index, value):
        red[s] = value

        def give(k, carry):
            remote(
                red.at[s], red.at[s], red_send.at[index], red_recv.at[index], (lax.rem(s + k, NS), t)
            ).start()
            return carry

        lax.fori_loop(1, NS, give, 0)

    def two_rows(first, second):
        row = lax.broadcasted_iota(jnp.int32, (8, LANES), 0)
        first = jnp.sum(first, axis=0, keepdims=True)
        second = jnp.sum(second, axis=0, keepdims=True)
        return jnp.where(row == 0, first, jnp.where(row == 1, second, 0.0))

    def collect(red, index):
        red_wait(red, index)
        total = red[0]
        for k in range(1, NS):
            total = total + red[k]
        return total

    spread(red_a, 0, two_rows(*sums))

    loads[2].wait()

    def back_one(i, carry):
        r = lax.div(i, per_rec)
        part = lax.rem(i, per_rec)
        row0 = pl.multiple_of(part * TM, TM)

        @pl.when(part == 0)
        def _():
            grads_load(r).wait()

        gn[r, pl.ds(row0 + EDGE, TM)] = mm(gv[r, pl.ds(row0, TM), :], wo[...])
        return carry

    lax.fori_loop(0, R * per_rec, back_one, 0)

    total = collect(red_a, 0)
    count = (lengths[0] + lengths[1] + lengths[2] + lengths[3]).astype(F32)
    inv_count = 1.0 / jnp.full((1, LANES), count, F32)
    centre = total[0:1] * inv_count
    spread_sq = total[1:2] * inv_count - centre * centre
    inv_std = lax.rsqrt(spread_sq + EPS)
    gain_row = gain[...]
    shift_row = shift[...]

    def norm_rec(r, sums):
        def norm_tile(i, sums):
            row0 = pl.multiple_of(i * TC, TC)
            rows = pl.ds(row0, TC)
            padded = pl.ds(row0 + EDGE, TC)
            unit = (cv[r, padded] - centre) * inv_std
            normalized = unit * gain_row + shift_row
            sig = jax.nn.sigmoid(normalized)
            ok = valid(r, row0, TC)
            sw[r, rows] = jnp.where(ok, normalized * sig, 0.0).astype(BF16)
            grad = gn[r, padded] * sig * (1.0 + normalized * (1.0 - sig))
            grad = jnp.where(ok, grad, 0.0)
            gn[r, padded] = grad
            return sums[0] + fold(grad), sums[1] + fold(grad * unit)

        sums = lax.fori_loop(0, tiles, norm_tile, sums)
        send_edges(2, gn, r)
        return sums

    sums = lax.fori_loop(0, R, norm_rec, (zero, zero))
    spread(red_b, 1, two_rows(*sums))

    own_pick = picker(x, core)

    def chunk_place(q):
        r = lax.div(q, cpr)
        return r, pl.multiple_of(lax.rem(q, cpr) * F, F)

    def out_weight_part(q, carry):
        r, row0 = chunk_place(q)
        rows = pl.ds(row0, F)
        woacc[...] += mm_tl(sw[r, rows, :], gv[r, rows, :])
        got[q] = mm_t(own_pick, gv[r, rows, :]).astype(BF16)
        return carry

    lax.fori_loop(0, NCH, out_weight_part, 0)

    def ship_weight(index, acc, first):
        for b in range(D // LANES):
            wsend[index, b * LANES : (b + 1) * LANES, :] = jnp.transpose(
                acc[first : first + LANES, b * LANES : (b + 1) * LANES]
            )

        def give(k, carry):
            p = lax.rem(s + k, NS)
            remote(
                wsend.at[index, pl.ds(pl.multiple_of(p * DP, DP), DP)],
                wrecv.at[index, s],
                wr_send.at[index],
                wr_recv.at[index],
                (p, t),
            ).start()
            return carry

        lax.fori_loop(1, NS, give, 0)
        wrecv[index, s] = wsend[index, pl.ds(pl.multiple_of(s * DP, DP), DP)]

    ship_weight(2, woacc, 0)

    total = collect(red_b, 1)
    gshift[...] = total[0:1]
    ggain[...] = total[1:2]
    scale = gain_row * inv_std
    mean_shift = total[0:1] * inv_count
    mean_gain = total[1:2] * inv_count

    padded_rows = NF + 2 * EDGE
    TE = padded_rows // 10 if padded_rows % 80 == 0 else 8

    def conv_grad_rec(r, carry):
        take_edges(1, cv, r)
        take_edges(2, gn, r)

        def conv_grad_tile(i, carry):
            row0 = pl.multiple_of(i * TE, TE)
            rows = pl.ds(row0, TE)
            unit = (cv[r, rows] - centre) * inv_std
            grad = scale * (gn[r, rows] - mean_shift - unit * mean_gain)
            gc[r, rows] = jnp.where(valid(r, row0 - EDGE, TE), grad, 0.0)
            return carry

        return lax.fori_loop(0, padded_rows // TE, conv_grad_tile, carry)

    lax.fori_loop(0, R, conv_grad_rec, 0)
    weight_swap.wait_recv()

    def swap_copy(q):
        return remote(gbuf.at[q], goth.at[q], ge_send.at[q], ge_recv.at[q], (s, other))

    def d2_copies(q):
        return (
            remote(s2.at[q, 0], r2.at[q, 0], d2_send.at[2 * q], d2_recv.at[2 * q], (s, right)),
            remote(
                s2.at[q, 1], r2.at[q, 1], d2_send.at[2 * q + 1], d2_recv.at[2 * q + 1], (s, left)
            ),
        )

    def nb_copies(q):
        return (
            remote(sx.at[q, 0], rx.at[q, 0], nb_send.at[2 * q], nb_recv.at[2 * q], (s, right)),
            remote(
                sx.at[q, 1], rx.at[q, 1], nb_send.at[2 * q + 1], nb_recv.at[2 * q + 1], (s, left)
            ),
        )

    def weight_rows(hop):
        return pl.ds(pl.multiple_of(lax.rem(x + hop, XN) * M, M), M)

    def partial(q, hop):
        rows = weight_rows(hop)
        return mm_t(wd_own[rows, :], gbuf[q]) + mm_t(wd_oth[rows, :], goth[q])

    def pointwise_grads(q):
        r, base = chunk_place(q)

        def tile(i, taps_sum):
            row0 = pl.multiple_of(base + i * TC, TC)
            rows = pl.ds(row0, TC)
            here = pl.ds(pl.multiple_of(i * TC, TC), TC)
            grad = tap_rows[0] * gc[r, pl.ds(row0 + EDGE + H, TC)]
            for k in range(1, K):
                grad = grad + tap_rows[k] * gc[r, pl.ds(row0 + EDGE + H - k, TC)]
            grad = jnp.where(valid(r, row0, TC), grad, 0.0)
            gbuf[q, here, 0:LANES] = (grad * gs[r, rows]).astype(BF16)
            gbuf[q, here, LANES : 2 * LANES] = (grad * a2[r, rows]).astype(BF16)
            centre_rows = gc[r, pl.ds(row0 + EDGE, TC)]
            return tuple(
                taps_sum[k] + fold(centre_rows * gp[r, pl.ds(row0 + EDGE - H + k, TC)])
                for k in range(K)
            )

        taps_sum = lax.fori_loop(0, F // TC, tile, tuple(tacc[k] for k in range(K)))
        for k in range(K):
            tacc[k] = taps_sum[k]

    def far_sends(q):
        swap_copy(q).wait_recv()
        far = partial(q, 2).astype(BF16)
        s2[q, 0] = far[:, :HF]
        s2[q, 1] = far[:, HF:]
        for copy in d2_copies(q):
            copy.start()

    def near_sends(q):
        to_right = partial(q, 1)
        to_left = partial(q, 3)
        from_left, from_right = d2_copies(q)
        from_left.wait_recv()
        sx[q, 0, :, :HF] = (to_right[:, :HF] + r2[q, 0].astype(F32)).astype(BF16)
        sx[q, 0, :, HF:] = to_right[:, HF:].astype(BF16)
        from_right.wait_recv()
        sx[q, 1, :, :HF] = to_left[:, :HF].astype(BF16)
        sx[q, 1, :, HF:] = (to_left[:, HF:] + r2[q, 1].astype(F32)).astype(BF16)
        for copy in nb_copies(q):
            copy.start()

    def out_place(q, owner):
        r, row0 = chunk_place(q)
        return gin.at[r, :, pl.ds(pl.multiple_of(owner * NF + row0, F), F)]

    def own_copy(q):
        return pltpu.make_async_copy(osend.at[q, s], out_place(q, s), aa_own.at[q])

    def finish(q):
        total = partial(q, 0) + got[q].astype(F32)
        for copy in nb_copies(q):
            copy.wait_recv()
        total = total + rx[q, 0].astype(F32) + rx[q, 1].astype(F32)
        osend[q] = total.astype(BF16).reshape(NS, 8, F)
        own_copy(q).start()

        def give(k, carry):
            p = lax.rem(s + k, NS)
            remote(
                osend.at[q, p], out_place(q, s), aa_send.at[q], aa_recv.at[q], (p, t)
            ).start()
            return carry

        lax.fori_loop(1, NS, give, 0)

    def weight_part(q):
        r, row0 = chunk_place(q)
        wacc[...] += mm_tl(gbuf[q], nv[r, pl.ds(row0, F), :])

    LAG_A, LAG_B, LAG_C = 1, 2, 4

    def step(i, carry):
        @pl.when(i < NCH)
        def _():
            pointwise_grads(i)
            swap_copy(i).start()

        @pl.when(jnp.logical_and(i >= LAG_A, i < NCH + LAG_A))
        def _():
            far_sends(i - LAG_A)

        @pl.when(i < NCH)
        def _():
            weight_part(i)

        @pl.when(i == NCH - 1)
        def _():
            for k in range(K):
                red_c[s, k : k + 1] = jnp.sum(tacc[k], axis=0, keepdims=True)

            def give(k, carry):
                remote(
                    red_c.at[s], red_c.at[s], red_send.at[2], red_recv.at[2], (lax.rem(s + k, NS), t)
                ).start()
                return carry

            lax.fori_loop(1, NS, give, 0)
            ship_weight(0, wacc, 0)
            ship_weight(1, wacc, LANES)

        @pl.when(jnp.logical_and(i >= LAG_B, i < NCH + LAG_B))
        def _():
            near_sends(i - LAG_B)

        @pl.when(i >= LAG_C)
        def _():
            finish(i - LAG_C)

        return carry

    for k in range(K, 16):
        red_c[s, k : k + 1] = jnp.zeros((1, LANES), F32)
    lax.fori_loop(0, NCH + LAG_C, step, 0)

    gtaps[...] = collect(red_c, 2)[0:K]

    for index, out in ((2, gwo), (0, gwv), (1, gwg)):
        slots = wrecv.at[index, pl.ds(0, NS - 1)]
        pltpu.make_async_copy(slots, slots, wr_recv.at[index]).wait()
        total = wrecv[index, 0]
        for k in range(1, NS):
            total = total + wrecv[index, k]
        out[...] = total

    weight_swap.wait_send()

    def edges_left(index, carry):
        part = halo.at[0, 0, 0]
        pltpu.make_async_copy(part, part, halo_send.at[index]).wait()
        return carry

    lax.fori_loop(0, 6 * R, edges_left, 0)
    red_sent(red_a, 0)
    red_sent(red_b, 1)
    red_sent(red_c, 2)
    for index in range(3):
        slots = wrecv.at[index, pl.ds(0, NS - 1)]
        pltpu.make_async_copy(slots, slots, wr_send.at[index]).wait()

    def drain(q, carry):
        swap_copy(q).wait_send()
        for copy in d2_copies(q):
            copy.wait_send()
        for copy in nb_copies(q):
            copy.wait_send()
        own_copy(q).wait()
        part = osend.at[q, pl.ds(0, NS - 1)]
        pltpu.make_async_copy(part, part, aa_send.at[q]).wait()
        pltpu.make_async_copy(part, part, aa_recv.at[q]).wait()
        return carry

    lax.fori_loop(0, NCH, drain, 0)


def per_device(
    normed,
    grad_out,
    value_weight,
    gate_weight,
    depth_taps,
    norm_gain,
    norm_shift,
    out_weight,
    lengths,
):
    R, NF, D = normed.shape
    K, CW = depth_taps.shape
    NS = lax.axis_size("seq")
    M = 8 * NS
    F = min(512, NF)
    TM = min(512, NF)
    TC = min(64, F)
    NCH = R * NF // F
    HF = F // 2
    DP = D // NS
    cfg = (R, NF, D, NS, F, TM, TC)
    vmem = pl.BlockSpec(memory_space=pltpu.VMEM)
    hbm = pl.BlockSpec(memory_space=pl.ANY)
    dma = pltpu.SemaphoreType.DMA
    padded = NF + 2 * EDGE
    out_shape = (
        jax.ShapeDtypeStruct((R, 8, NS * NF), BF16),
        jax.ShapeDtypeStruct((DP, CW), F32),
        jax.ShapeDtypeStruct((DP, CW), F32),
        jax.ShapeDtypeStruct((DP, CW), F32),
        jax.ShapeDtypeStruct((K, CW), F32),
        jax.ShapeDtypeStruct((1, CW), F32),
        jax.ShapeDtypeStruct((1, CW), F32),
    )
    scratch = [
        pltpu.VMEM((R, NF, D), BF16),
        pltpu.VMEM((R, NF, D), BF16),
        pltpu.VMEM((D, 2 * LANES), BF16),
        pltpu.VMEM((D, LANES), BF16),
        pltpu.VMEM((XN * M, 2 * LANES), BF16),
        pltpu.VMEM((XN * M, 2 * LANES), BF16),
        pltpu.VMEM((XN * M, 2 * LANES), BF16),
        pltpu.VMEM((R, padded, LANES), F32),
        pltpu.VMEM((R, NF, LANES), F32),
        pltpu.VMEM((R, NF, LANES), F32),
        pltpu.VMEM((R, padded, LANES), F32),
        pltpu.VMEM((R, padded, LANES), F32),
        pltpu.VMEM((R, padded, LANES), F32),
        pltpu.VMEM((R, NF, LANES), BF16),
        pltpu.VMEM((3, R, 2, EDGE, LANES), F32),
        pltpu.VMEM((NS, 8, LANES), F32),
        pltpu.VMEM((NS, 8, LANES), F32),
        pltpu.VMEM((NS, 16, LANES), F32),
        pltpu.VMEM((NCH, M, F), BF16),
        pltpu.VMEM((NCH, F, 2 * LANES), BF16),
        pltpu.VMEM((NCH, F, 2 * LANES), BF16),
        pltpu.VMEM((NCH, 2, M, HF), BF16),
        pltpu.VMEM((NCH, 2, M, HF), BF16),
        pltpu.VMEM((NCH, 2, M, F), BF16),
        pltpu.VMEM((NCH, 2, M, F), BF16),
        pltpu.VMEM((NCH, NS, 8, F), BF16),
        pltpu.VMEM((K, 8, LANES), F32),
        pltpu.VMEM((2 * LANES, D), F32),
        pltpu.VMEM((LANES, D), F32),
        pltpu.VMEM((3, D, LANES), F32),
        pltpu.VMEM((3, NS, DP, LANES), F32),
        dma((3 + 2 * R,)),
        dma((6 * R,)),
        dma((6 * R,)),
        dma((3,)),
        dma((3,)),
        dma,
        dma,
        dma((NCH,)),
        dma((NCH,)),
        dma((2 * NCH,)),
        dma((2 * NCH,)),
        dma((2 * NCH,)),
        dma((2 * NCH,)),
        dma((NCH,)),
        dma((NCH,)),
        dma((NCH,)),
        dma((3,)),
        dma((3,)),
    ]
    outs = pl.pallas_call(
        functools.partial(kernel, cfg),
        out_shape=out_shape,
        in_specs=[pl.BlockSpec(memory_space=pltpu.SMEM)] + [hbm] * 5 + [vmem] * 3,
        out_specs=(hbm,) + (vmem,) * 6,
        scratch_shapes=scratch,
        compiler_params=pltpu.CompilerParams(
            collective_id=0, has_side_effects=True, vmem_limit_bytes=60 * 1024 * 1024
        ),
        cost_estimate=pl.CostEstimate(
            flops=8 * 2 * R * NF * D * CW, bytes_accessed=4 * R * NF * D, transcendentals=0
        ),
    )(
        lengths,
        normed,
        grad_out,
        value_weight,
        gate_weight,
        out_weight,
        depth_taps,
        norm_gain.reshape(1, CW),
        norm_shift.reshape(1, CW),
    )
    grad_in, grad_wv, grad_wg, grad_wo, grad_taps, grad_gain, grad_shift = outs
    return (
        grad_in,
        grad_wv,
        grad_wg,
        grad_wo,
        grad_taps,
        grad_gain.reshape(CW),
        grad_shift.reshape(CW),
    )


def solution(mesh):
    placed = (
        P(None, "seq", None),
        P(None, "seq", None),
        P(None, "tp"),
        P(None, "tp"),
        P(None, "tp"),
        P("tp"),
        P("tp"),
        P(None, "tp"),
        P(),
    )
    return jax.shard_map(
        per_device,
        mesh=mesh,
        in_specs=placed,
        out_specs=(
            P(None, ("seq", "tp"), None),
            P("seq", "tp"),
            P("seq", "tp"),
            P("seq", "tp"),
            P(None, "tp"),
            P("tp"),
            P("tp"),
        ),
        check_vma=False,
    )
```

```python
import functools

import jax
import jax.numpy as jnp
from jax import lax
from jax.experimental import pallas as pl
from jax.experimental.pallas import tpu as pltpu
from jax.sharding import PartitionSpec as P

MESH = pl.DeviceIdType.MESH
F32 = jnp.float32
BF16 = jnp.bfloat16
EPS = 1e-05
LANES = 128
EDGE = 8
PAD = 16
XN = 4


def mm(a, b):
    return jnp.dot(a, b, preferred_element_type=F32)


def mm_t(a, b):
    return lax.dot_general(a, b, (((1,), (1,)), ((), ())), preferred_element_type=F32)


def mm_tl(a, b):
    return lax.dot_general(a, b, (((0,), (0,)), ((), ())), preferred_element_type=F32)


def fold(v):
    rows = v.shape[0]
    return jnp.sum(v.reshape(rows // 8, 8, LANES), axis=0)


def kernel(
    cfg,
    lengths,
    normed_h,
    grads_h,
    wv_h,
    wg_h,
    wo_h,
    taps,
    gain,
    shift,
    gin,
    gwv,
    gwg,
    gwo,
    gtaps,
    ggain,
    gshift,
    nv,
    gv,
    wcat,
    wo,
    w_next,
    pick_own,
    wd,
    wd_send,
    gp,
    gs,
    a2,
    cv,
    gn,
    gc,
    sw,
    halo_out,
    halo,
    red_a,
    red_b,
    red_c,
    gg_out,
    gg_in,
    gmine,
    gother,
    far_out,
    far_in,
    osend,
    tacc,
    wacc,
    woacc,
    wsend,
    wrecv,
    load_sem,
    halo_send,
    halo_recv,
    red_send,
    red_recv,
    wx_send,
    wx_recv,
    wn_send,
    wn_recv,
    ge_send,
    ge_recv,
    gg_send,
    gg_recv,
    fr_send,
    fr_recv,
    aa_send,
    aa_recv,
    aa_own,
    wr_send,
    wr_recv,
):
    R, NF, D, NS, F, TM, TC = cfg
    K = taps.shape[0]
    H = (K - 1) // 2
    M = 8 * NS
    NCH = R * NF // F
    cpr = NF // F
    DP = D // NS
    s = lax.axis_index("seq")
    t = lax.axis_index("tp")
    x = lax.div(t, 2)
    core = lax.rem(t, 2)
    other = x * 2 + (1 - core)
    step = 1 - 2 * lax.rem(x, 2)
    x_far = lax.rem(x + XN - step, XN)
    pair = (x + step) * 2 + core
    far = x_far * 2 + core
    up = lax.rem(s + 1, NS)
    down = lax.rem(s + NS - 1, NS)

    barrier = pltpu.get_barrier_semaphore()

    def greet(k, carry):
        pl.semaphore_signal(
            barrier, inc=1, device_id=(lax.rem(s + k, NS), t), device_id_type=MESH
        )
        return carry

    lax.fori_loop(1, NS, greet, 0)
    for mate in (other, pair, far):
        pl.semaphore_signal(barrier, inc=1, device_id=(s, mate), device_id_type=MESH)

    loads = [
        pltpu.make_async_copy(wv_h, wcat.at[:, 0:LANES], load_sem.at[0]),
        pltpu.make_async_copy(wg_h, wcat.at[:, LANES : 2 * LANES], load_sem.at[1]),
        pltpu.make_async_copy(wo_h, wo, load_sem.at[2]),
    ]
    for load in loads:
        load.start()

    def normed_load(r):
        return pltpu.make_async_copy(normed_h.at[r], nv.at[r], load_sem.at[3 + r])

    def grads_load(r):
        return pltpu.make_async_copy(grads_h.at[r], gv.at[r], load_sem.at[3 + R + r])

    for r in range(R):
        normed_load(r).start()

    def valid(r, row0, rows):
        at = s * NF + row0 + lax.broadcasted_iota(jnp.int32, (rows, LANES), 0)
        return jnp.logical_and(at >= 0, at < lengths[r])

    def picker(xd, cd):
        row = lax.broadcasted_iota(jnp.int32, (M, D), 0)
        col = lax.broadcasted_iota(jnp.int32, (M, D), 1)
        want = (row // 8) * 64 + xd * 16 + cd * 8 + row % 8
        return jnp.where(col == want, 1.0, 0.0).astype(BF16)

    loads[0].wait()
    loads[1].wait()

    def pick_weights(source, group):
        for side, xd in enumerate((x, x_far)):
            rows = slice(side * M, (side + 1) * M)
            wd[group, rows] = mm(picker(xd, core), source[...]).astype(BF16)
            wd_send[group, rows] = mm(picker(xd, 1 - core), source[...]).astype(BF16)

    def weight_swap(group):
        return remote(
            wd_send.at[group],
            wd.at[2 + group],
            wx_send.at[group],
            wx_recv.at[group],
            (s, other),
        )

    tacc[...] = jnp.zeros_like(tacc)
    wacc[...] = jnp.zeros_like(wacc)
    woacc[...] = jnp.zeros_like(woacc)
    for r in range(R):
        gp[r, 0 : PAD - EDGE] = jnp.zeros((PAD - EDGE, LANES), F32)
        gp[r, NF + PAD + EDGE : NF + 2 * PAD] = jnp.zeros((PAD - EDGE, LANES), F32)

    def remote(src, dst, send, recv, device):
        return pltpu.make_async_remote_copy(
            src_ref=src,
            dst_ref=dst,
            send_sem=send,
            recv_sem=recv,
            device_id=device,
            device_id_type=MESH,
        )

    def edge_copies(kind):
        return (
            remote(
                halo_out.at[kind, 0],
                halo.at[kind, 0],
                halo_send.at[2 * kind],
                halo_recv.at[2 * kind],
                (up, t),
            ),
            remote(
                halo_out.at[kind, 1],
                halo.at[kind, 1],
                halo_send.at[2 * kind + 1],
                halo_recv.at[2 * kind + 1],
                (down, t),
            ),
        )

    def send_edges(kind, field):
        for r in range(R):
            halo_out[kind, 0, r] = field[r, PAD + NF - EDGE : PAD + NF]
            halo_out[kind, 1, r] = field[r, PAD : PAD + EDGE]
        for copy in edge_copies(kind):
            copy.start()

    def take_edges(kind, field):
        for copy in edge_copies(kind):
            copy.wait_recv()
        for r in range(R):
            field[r, PAD - EDGE : PAD] = jnp.where(s > 0, halo[kind, 0, r], 0.0)
            field[r, PAD + NF : PAD + NF + EDGE] = jnp.where(s < NS - 1, halo[kind, 1, r], 0.0)

    per_rec = NF // TM

    def forward(i, carry):
        r = lax.div(i, per_rec)
        part = lax.rem(i, per_rec)
        row0 = pl.multiple_of(part * TM, TM)
        rows = pl.ds(row0, TM)

        @pl.when(part == 0)
        def _():
            normed_load(r).wait()
            grads_load(r).start()

        both = mm(nv[r, rows, :], wcat[...])
        gate = jax.nn.sigmoid(both[:, LANES:])
        unit = both[:, :LANES] * gate
        gp[r, pl.ds(row0 + PAD, TM)] = jnp.where(valid(r, row0, TM), unit, 0.0)
        gs[r, rows] = gate
        a2[r, rows] = unit * (1.0 - gate)
        return carry

    lax.fori_loop(0, R * per_rec, forward, 0)
    pl.semaphore_wait(barrier, NS - 1 + 3)
    send_edges(0, gp)
    next_weights = remote(wcat, w_next, wn_send, wn_recv, (s, pair))
    next_weights.start()

    tap_rows = [taps[k : k + 1, :] for k in range(K)]
    tiles = NF // TC
    zero = jnp.zeros((8, LANES), F32)

    def conv_at(r, start, rows):
        total = tap_rows[0] * gp[r, pl.ds(start + PAD - H, rows)]
        for k in range(1, K):
            total = total + tap_rows[k] * gp[r, pl.ds(start + PAD - H + k, rows)]
        return total

    def conv_tile(r, i, sums):
        row0 = pl.multiple_of(i * TC, TC)
        total = conv_at(r, row0, TC)
        cv[r, pl.ds(row0 + PAD, TC)] = total
        kept = jnp.where(valid(r, row0, TC), total, 0.0)
        return sums[0] + fold(kept), sums[1] + fold(kept * kept)

    def conv_inner(r, sums):
        return lax.fori_loop(1, tiles - 1, functools.partial(conv_tile, r), sums)

    sums = lax.fori_loop(0, R, conv_inner, (zero, zero))
    loads[2].wait()

    def back_one(i, carry):
        r = lax.div(i, per_rec)
        part = lax.rem(i, per_rec)
        row0 = pl.multiple_of(part * TM, TM)

        @pl.when(part == 0)
        def _():
            grads_load(r).wait()

        gn[r, pl.ds(row0 + PAD, TM)] = mm(gv[r, pl.ds(row0, TM), :], wo[...])
        return carry

    lax.fori_loop(0, per_rec, back_one, 0)
    take_edges(0, gp)

    def conv_outer(r, sums):
        sums = conv_tile(r, 0, sums)
        return conv_tile(r, tiles - 1, sums)

    sums = lax.fori_loop(0, R, conv_outer, sums)

    def red_wait(red, index):
        part = red.at[pl.ds(0, NS - 1)]
        pltpu.make_async_copy(part, part, red_recv.at[index]).wait()

    def red_sent(red, index):
        part = red.at[pl.ds(0, NS - 1)]
        pltpu.make_async_copy(part, part, red_send.at[index]).wait()

    def spread_from(red, index):
        def give(k, carry):
            remote(
                red.at[s], red.at[s], red_send.at[index], red_recv.at[index], (lax.rem(s + k, NS), t)
            ).start()
            return carry

        lax.fori_loop(1, NS, give, 0)

    def spread(red, index, value):
        red[s] = value
        spread_from(red, index)

    def two_rows(first, second):
        row = lax.broadcasted_iota(jnp.int32, (8, LANES), 0)
        first = jnp.sum(first, axis=0, keepdims=True)
        second = jnp.sum(second, axis=0, keepdims=True)
        return jnp.where(row == 0, first, jnp.where(row == 1, second, 0.0))

    def collect(red, index):
        red_wait(red, index)
        total = red[0]
        for k in range(1, NS):
            total = total + red[k]
        return total

    spread(red_a, 0, two_rows(*sums))

    for r in range(R):
        cv[r, PAD - EDGE : PAD] = conv_at(r, -EDGE, EDGE)
        cv[r, PAD + NF : PAD + NF + EDGE] = conv_at(r, NF, EDGE)
    def chunk_place(q):
        r = lax.div(q, cpr)
        return r, pl.multiple_of(lax.rem(q, cpr) * F, F)

    lax.fori_loop(per_rec, R * per_rec, back_one, 0)
    pick_weights(wcat, 0)
    weight_swap(0).start()
    pick_own[...] = picker(x, core)

    total = collect(red_a, 0)
    count = (lengths[0] + lengths[1] + lengths[2] + lengths[3]).astype(F32)
    inv_count = 1.0 / jnp.full((1, LANES), count, F32)
    centre = total[0:1] * inv_count
    spread_sq = total[1:2] * inv_count - centre * centre
    inv_std = lax.rsqrt(spread_sq + EPS)
    gain_row = gain[...]
    shift_row = shift[...]

    def norm_rec(r, sums):
        def norm_tile(i, sums):
            row0 = pl.multiple_of(i * TC, TC)
            rows = pl.ds(row0, TC)
            padded = pl.ds(row0 + PAD, TC)
            unit = (cv[r, padded] - centre) * inv_std
            normalized = unit * gain_row + shift_row
            sig = jax.nn.sigmoid(normalized)
            ok = valid(r, row0, TC)
            sw[r, rows] = jnp.where(ok, normalized * sig, 0.0).astype(BF16)
            grad = gn[r, padded] * sig * (1.0 + normalized * (1.0 - sig))
            grad = jnp.where(ok, grad, 0.0)
            gn[r, padded] = grad
            return sums[0] + fold(grad), sums[1] + fold(grad * unit)

        return lax.fori_loop(0, tiles, norm_tile, sums)

    sums = lax.fori_loop(0, R, norm_rec, (zero, zero))
    spread(red_b, 1, two_rows(*sums))
    send_edges(1, gn)

    def out_weight_part(q, carry):
        r, row0 = chunk_place(q)
        rows = pl.ds(row0, F)
        woacc[...] += mm_tl(sw[r, rows, :], gv[r, rows, :])
        return carry

    lax.fori_loop(0, NCH, out_weight_part, 0)

    def turn_weight(index, acc, first):
        for b in range(D // LANES):
            wsend[index, b * LANES : (b + 1) * LANES, :] = jnp.transpose(
                acc[first : first + LANES, b * LANES : (b + 1) * LANES]
            )

    def ship_weight(index):
        def give(k, carry):
            p = lax.rem(s + k, NS)
            remote(
                wsend.at[index, pl.ds(pl.multiple_of(p * DP, DP), DP)],
                wrecv.at[index, s],
                wr_send.at[index],
                wr_recv.at[index],
                (p, t),
            ).start()
            return carry

        lax.fori_loop(1, NS, give, 0)
        wrecv[index, s] = wsend[index, pl.ds(pl.multiple_of(s * DP, DP), DP)]

    turn_weight(2, woacc, 0)
    next_weights.wait_recv()
    pick_weights(w_next, 1)
    weight_swap(1).start()
    total = collect(red_b, 1)
    ship_weight(2)
    gshift[...] = total[0:1]
    ggain[...] = total[1:2]
    scale = gain_row * inv_std
    mean_shift = total[0:1] * inv_count
    mean_gain = total[1:2] * inv_count

    take_edges(1, gn)
    padded_rows = NF + 2 * EDGE
    TE = padded_rows // 10 if padded_rows % 80 == 0 else 8

    def conv_grad(r):
        def conv_grad_tile(i, carry):
            row0 = pl.multiple_of(i * TE, TE)
            rows = pl.ds(row0 + PAD - EDGE, TE)
            unit = (cv[r, rows] - centre) * inv_std
            grad = scale * (gn[r, rows] - mean_shift - unit * mean_gain)
            gc[r, rows] = jnp.where(valid(r, row0 - EDGE, TE), grad, 0.0)
            return carry

        lax.fori_loop(0, padded_rows // TE, conv_grad_tile, 0)

    def swap_copy(q, group):
        index = 2 * q + group
        return remote(
            gmine.at[q, group],
            gother.at[q, group],
            ge_send.at[index],
            ge_recv.at[index],
            (s, other),
        )

    def pair_copy(q):
        return remote(gg_out.at[q], gg_in.at[q], gg_send.at[q], gg_recv.at[q], (s, pair))

    def far_copy(q):
        return remote(far_out.at[q], far_in.at[q], fr_send.at[q], fr_recv.at[q], (s, far))

    def partial(q, side):
        rows = slice(side * M, (side + 1) * M)
        total = mm_t(wd[0, rows], gmine[q, 0]) + mm_t(wd[1, rows], gmine[q, 1])
        return total + (mm_t(wd[2, rows], gother[q, 0]) + mm_t(wd[3, rows], gother[q, 1]))

    def pointwise_grads(q):
        r, base = chunk_place(q)

        def tile(i, taps_sum):
            row0 = pl.multiple_of(base + i * TC, TC)
            rows = pl.ds(row0, TC)
            here = pl.ds(pl.multiple_of(i * TC, TC), TC)
            grad = tap_rows[0] * gc[r, pl.ds(row0 + PAD + H, TC)]
            for k in range(1, K):
                grad = grad + tap_rows[k] * gc[r, pl.ds(row0 + PAD + H - k, TC)]
            grad = jnp.where(valid(r, row0, TC), grad, 0.0)
            gg_out[q, here] = grad.astype(BF16)
            gmine[q, 0, here, 0:LANES] = (grad * gs[r, rows]).astype(BF16)
            gmine[q, 0, here, LANES : 2 * LANES] = (grad * a2[r, rows]).astype(BF16)
            centre_rows = gc[r, pl.ds(row0 + PAD, TC)]
            return tuple(
                taps_sum[k] + fold(centre_rows * gp[r, pl.ds(row0 + PAD - H + k, TC)])
                for k in range(K)
            )

        taps_sum = lax.fori_loop(0, F // TC, tile, tuple(tacc[k] for k in range(K)))
        for k in range(K):
            tacc[k] = taps_sum[k]

    def pair_grads(q):
        r, row0 = chunk_place(q)
        both = mm(nv[r, pl.ds(row0, F), :], w_next[...])
        gate = jax.nn.sigmoid(both[:, LANES:])
        unit = both[:, :LANES] * gate
        pair_copy(q).wait_recv()
        grad = gg_in[q].astype(F32)
        gmine[q, 1, :, 0:LANES] = (grad * gate).astype(BF16)
        gmine[q, 1, :, LANES : 2 * LANES] = (grad * (unit * (1.0 - gate))).astype(BF16)
        swap_copy(q, 1).start()

    def far_sends(q):
        for group in range(2):
            swap_copy(q, group).wait_recv()
        far_out[q] = partial(q, 1).astype(BF16)
        far_copy(q).start()

    def out_place(q, owner):
        r, row0 = chunk_place(q)
        return gin.at[r, :, pl.ds(pl.multiple_of(owner * NF + row0, F), F)]

    def own_copy(q):
        return pltpu.make_async_copy(osend.at[q, s], out_place(q, s), aa_own.at[q])

    def finish(q):
        r, row0 = chunk_place(q)
        total = partial(q, 0) + mm_t(pick_own[...], gv[r, pl.ds(row0, F), :])
        far_copy(q).wait_recv()
        total = total + far_in[q].astype(F32)
        osend[q] = total.astype(BF16).reshape(NS, 8, F)
        own_copy(q).start()

        def give(k, carry):
            p = lax.rem(s + k, NS)
            remote(
                osend.at[q, p], out_place(q, s), aa_send.at[q], aa_recv.at[q], (p, t)
            ).start()
            return carry

        lax.fori_loop(1, NS, give, 0)

    def weight_part(q):
        r, row0 = chunk_place(q)
        wacc[...] += mm_tl(gmine[q, 0], nv[r, pl.ds(row0, F), :])

    for k in range(K, 16):
        red_c[s, k : k + 1] = jnp.zeros((1, LANES), F32)

    LATE = NCH // 4

    def outward(i, carry):
        @pl.when(lax.rem(i, cpr) == 0)
        def _():
            conv_grad(lax.div(i, cpr))

        pointwise_grads(i)
        pair_copy(i).start()
        swap_copy(i, 0).start()

        @pl.when(i < NCH - 2 * LATE)
        def _():
            weight_part(i)

        return carry

    lax.fori_loop(0, NCH, outward, 0)
    for group in range(2):
        weight_swap(group).wait_recv()

    LAG_B, LAG_C = 1, 3

    def homeward(i, carry):
        @pl.when(i < NCH)
        def _():
            pair_grads(i)

        @pl.when(jnp.logical_and(i >= LAG_B, i < NCH + LAG_B))
        def _():
            far_sends(i - LAG_B)

        @pl.when(i < LATE)
        def _():
            weight_part(NCH - 2 * LATE + 2 * i)
            weight_part(NCH - 2 * LATE + 2 * i + 1)

        @pl.when(i == LATE - 1)
        def _():
            for index in range(2):
                turn_weight(index, wacc, index * LANES)
                ship_weight(index)
            for k in range(K):
                red_c[s, k : k + 1] = jnp.sum(tacc[k], axis=0, keepdims=True)
            spread_from(red_c, 2)

        @pl.when(i >= LAG_C)
        def _():
            finish(i - LAG_C)

        return carry

    lax.fori_loop(0, NCH + LAG_C, homeward, 0)

    gtaps[...] = collect(red_c, 2)[0:K]

    for index, out in ((2, gwo), (0, gwv), (1, gwg)):
        slots = wrecv.at[index, pl.ds(0, NS - 1)]
        pltpu.make_async_copy(slots, slots, wr_recv.at[index]).wait()
        total = wrecv[index, 0]
        for k in range(1, NS):
            total = total + wrecv[index, k]
        out[...] = total

    next_weights.wait_send()
    for group in range(2):
        weight_swap(group).wait_send()

    for kind in range(2):
        for copy in edge_copies(kind):
            copy.wait_send()
    red_sent(red_a, 0)
    red_sent(red_b, 1)
    red_sent(red_c, 2)
    for index in range(3):
        slots = wrecv.at[index, pl.ds(0, NS - 1)]
        pltpu.make_async_copy(slots, slots, wr_send.at[index]).wait()

    def drain(q, carry):
        for group in range(2):
            swap_copy(q, group).wait_send()
        pair_copy(q).wait_send()
        far_copy(q).wait_send()
        own_copy(q).wait()
        part = osend.at[q, pl.ds(0, NS - 1)]
        pltpu.make_async_copy(part, part, aa_send.at[q]).wait()
        pltpu.make_async_copy(part, part, aa_recv.at[q]).wait()
        return carry

    lax.fori_loop(0, NCH, drain, 0)


def hand_on(*refs):
    half = (len(refs) - 1) // 2
    sems = refs[-1]
    copies = [pltpu.make_async_copy(refs[i], refs[half + i], sems.at[i]) for i in range(half)]
    for copy in copies:
        copy.start()
    for copy in copies:
        copy.wait()


def per_device(
    normed,
    grad_out,
    value_weight,
    gate_weight,
    depth_taps,
    norm_gain,
    norm_shift,
    out_weight,
    lengths,
):
    R, NF, D = normed.shape
    K, CW = depth_taps.shape
    NS = lax.axis_size("seq")
    M = 8 * NS
    F = min(512, NF)
    TM = min(512, NF)
    TC = min(64, F)
    NCH = R * NF // F
    DP = D // NS
    cfg = (R, NF, D, NS, F, TM, TC)
    vmem = pl.BlockSpec(memory_space=pltpu.VMEM)
    hbm = pl.BlockSpec(memory_space=pl.ANY)
    dma = pltpu.SemaphoreType.DMA
    padded = NF + 2 * PAD
    out_shape = (
        jax.ShapeDtypeStruct((R, 8, NS * NF), BF16),
        jax.ShapeDtypeStruct((DP, CW), F32),
        jax.ShapeDtypeStruct((DP, CW), F32),
        jax.ShapeDtypeStruct((DP, CW), F32),
        jax.ShapeDtypeStruct((K, CW), F32),
        jax.ShapeDtypeStruct((1, CW), F32),
        jax.ShapeDtypeStruct((1, CW), F32),
    )
    scratch = [
        pltpu.VMEM((R, NF, D), BF16),
        pltpu.VMEM((R, NF, D), BF16),
        pltpu.VMEM((D, 2 * LANES), BF16),
        pltpu.VMEM((D, LANES), BF16),
        pltpu.VMEM((D, 2 * LANES), BF16),
        pltpu.VMEM((M, D), BF16),
        pltpu.VMEM((4, 2 * M, 2 * LANES), BF16),
        pltpu.VMEM((2, 2 * M, 2 * LANES), BF16),
        pltpu.VMEM((R, padded, LANES), F32),
        pltpu.VMEM((R, NF, LANES), F32),
        pltpu.VMEM((R, NF, LANES), F32),
        pltpu.VMEM((R, padded, LANES), F32),
        pltpu.VMEM((R, padded, LANES), F32),
        pltpu.VMEM((R, padded, LANES), F32),
        pltpu.VMEM((R, NF, LANES), BF16),
        pltpu.VMEM((2, 2, R, EDGE, LANES), F32),
        pltpu.VMEM((2, 2, R, EDGE, LANES), F32),
        pltpu.VMEM((NS, 8, LANES), F32),
        pltpu.VMEM((NS, 8, LANES), F32),
        pltpu.VMEM((NS, 16, LANES), F32),
        pltpu.VMEM((NCH, F, LANES), BF16),
        pltpu.VMEM((NCH, F, LANES), BF16),
        pltpu.VMEM((NCH, 2, F, 2 * LANES), BF16),
        pltpu.VMEM((NCH, 2, F, 2 * LANES), BF16),
        pltpu.VMEM((NCH, M, F), BF16),
        pltpu.VMEM((NCH, M, F), BF16),
        pltpu.VMEM((NCH, NS, 8, F), BF16),
        pltpu.VMEM((K, 8, LANES), F32),
        pltpu.VMEM((2 * LANES, D), F32),
        pltpu.VMEM((LANES, D), F32),
        pltpu.VMEM((3, D, LANES), F32),
        pltpu.VMEM((3, NS, DP, LANES), F32),
        dma((3 + 2 * R,)),
        dma((4,)),
        dma((4,)),
        dma((3,)),
        dma((3,)),
        dma((2,)),
        dma((2,)),
        dma,
        dma,
        dma((2 * NCH,)),
        dma((2 * NCH,)),
        dma((NCH,)),
        dma((NCH,)),
        dma((NCH,)),
        dma((NCH,)),
        dma((NCH,)),
        dma((NCH,)),
        dma((NCH,)),
        dma((3,)),
        dma((3,)),
    ]
    outs = pl.pallas_call(
        functools.partial(kernel, cfg),
        out_shape=tuple(pltpu.VMEM(o.shape, o.dtype) for o in out_shape),
        in_specs=[pl.BlockSpec(memory_space=pltpu.SMEM)] + [hbm] * 5 + [vmem] * 3,
        out_specs=(vmem,) * 7,
        scratch_shapes=scratch,
        compiler_params=pltpu.CompilerParams(
            collective_id=0, has_side_effects=True, vmem_limit_bytes=60 * 1024 * 1024
        ),
        cost_estimate=pl.CostEstimate(
            flops=8 * 2 * R * NF * D * CW, bytes_accessed=4 * R * NF * D, transcendentals=0
        ),
    )(
        lengths,
        normed,
        grad_out,
        value_weight,
        gate_weight,
        out_weight,
        depth_taps,
        norm_gain.reshape(1, CW),
        norm_shift.reshape(1, CW),
    )
    held = [pltpu.with_memory_space_constraint(o, pltpu.VMEM) for o in outs]
    moved = pl.pallas_call(
        hand_on,
        out_shape=out_shape,
        in_specs=[vmem] * len(out_shape),
        out_specs=(hbm,) * len(out_shape),
        scratch_shapes=[dma((len(out_shape),))],
    )(*held)
    grad_in, grad_wv, grad_wg, grad_wo, grad_taps, grad_gain, grad_shift = moved
    return (
        grad_in,
        grad_wv,
        grad_wg,
        grad_wo,
        grad_taps,
        grad_gain.reshape(CW),
        grad_shift.reshape(CW),
    )


def solution(mesh):
    placed = (
        P(None, "seq", None),
        P(None, "seq", None),
        P(None, "tp"),
        P(None, "tp"),
        P(None, "tp"),
        P("tp"),
        P("tp"),
        P(None, "tp"),
        P(),
    )
    return jax.shard_map(
        per_device,
        mesh=mesh,
        in_specs=placed,
        out_specs=(
            P(None, ("seq", "tp"), None),
            P("seq", "tp"),
            P("seq", "tp"),
            P("seq", "tp"),
            P(None, "tp"),
            P("tp"),
            P("tp"),
        ),
        check_vma=False,
    )
```

```python
import functools

import jax
import jax.numpy as jnp
from jax import lax
from jax.experimental import pallas as pl
from jax.experimental.pallas import tpu as pltpu
from jax.sharding import PartitionSpec as P

MESH = pl.DeviceIdType.MESH
F32 = jnp.float32
BF16 = jnp.bfloat16
EPS = 1e-05
LANES = 128
EDGE = 8
PAD = 16
XN = 4


def mm(a, b):
    return jnp.dot(a, b, preferred_element_type=F32)


def mm_t(a, b):
    return lax.dot_general(a, b, (((1,), (1,)), ((), ())), preferred_element_type=F32)


def mm_tl(a, b):
    return lax.dot_general(a, b, (((0,), (0,)), ((), ())), preferred_element_type=F32)


def fold(v):
    rows = v.shape[0]
    return jnp.sum(v.reshape(rows // 8, 8, LANES), axis=0)


def kernel(
    cfg,
    lengths,
    normed_h,
    grads_h,
    wv_h,
    wg_h,
    wo_h,
    taps,
    gain,
    shift,
    gin,
    gwv,
    gwg,
    gwo,
    gtaps,
    ggain,
    gshift,
    nv,
    gv,
    wcat,
    wo,
    w_next,
    wd,
    wd_send,
    wd_oth,
    feats,
    own_part,
    gp,
    gs,
    a2,
    cv,
    gn,
    gc,
    sw,
    halo_out,
    halo,
    red_a,
    red_b,
    red_c,
    gg_out,
    gg_in,
    gmine,
    gother,
    far_out,
    far_in,
    osend,
    tacc,
    wacc,
    woacc,
    wsend,
    wrecv,
    load_sem,
    halo_send,
    halo_recv,
    red_send,
    red_recv,
    wx_send,
    wx_recv,
    wn_send,
    wn_recv,
    ge_send,
    ge_recv,
    gg_send,
    gg_recv,
    fr_send,
    fr_recv,
    aa_send,
    aa_recv,
    aa_own,
    wr_send,
    wr_recv,
):
    R, NF, D, NS, F, TM, TC = cfg
    K = taps.shape[0]
    H = (K - 1) // 2
    M = 8 * NS
    NCH = R * NF // F
    cpr = NF // F
    DP = D // NS
    s = lax.axis_index("seq")
    t = lax.axis_index("tp")
    x = lax.div(t, 2)
    core = lax.rem(t, 2)
    other = x * 2 + (1 - core)
    step = 1 - 2 * lax.rem(x, 2)
    x_pair = (x + step, lax.rem(x + XN - step, XN))
    pair = tuple(xp * 2 + core for xp in x_pair)
    up = lax.rem(s + 1, NS)
    down = lax.rem(s + NS - 1, NS)

    barrier = pltpu.get_barrier_semaphore()

    def greet(k, carry):
        pl.semaphore_signal(
            barrier, inc=1, device_id=(lax.rem(s + k, NS), t), device_id_type=MESH
        )
        return carry

    lax.fori_loop(1, NS, greet, 0)
    for mate in (other,) + pair:
        pl.semaphore_signal(barrier, inc=1, device_id=(s, mate), device_id_type=MESH)

    loads = [
        pltpu.make_async_copy(wv_h, wcat.at[:, 0:LANES], load_sem.at[0]),
        pltpu.make_async_copy(wg_h, wcat.at[:, LANES : 2 * LANES], load_sem.at[1]),
        pltpu.make_async_copy(wo_h, wo.at[:, 0:LANES], load_sem.at[2]),
    ]
    for load in loads:
        load.start()

    def normed_load(r):
        return pltpu.make_async_copy(normed_h.at[r], nv.at[r], load_sem.at[3 + r])

    def grads_load(r):
        return pltpu.make_async_copy(grads_h.at[r], gv.at[r], load_sem.at[3 + R + r])

    for r in range(R):
        normed_load(r).start()

    def valid(r, row0, rows):
        at = s * NF + row0 + lax.broadcasted_iota(jnp.int32, (rows, LANES), 0)
        return jnp.logical_and(at >= 0, at < lengths[r])

    def picker(xd, cd):
        row = lax.broadcasted_iota(jnp.int32, (M, D), 0)
        col = lax.broadcasted_iota(jnp.int32, (M, D), 1)
        want = (row // 8) * 64 + xd * 16 + cd * 8 + row % 8
        return jnp.where(col == want, 1.0, 0.0).astype(BF16)

    feature = lax.broadcasted_iota(jnp.int32, (D, LANES), 0)
    place = lax.broadcasted_iota(jnp.int32, (D, LANES), 1)
    want = (place // 8) * 64 + x * 16 + core * 8 + place % 8
    wo[:, LANES : 2 * LANES] = jnp.where(
        jnp.logical_and(feature == want, place < M), 1.0, 0.0
    ).astype(BF16)
    loads[0].wait()
    loads[1].wait()

    def pick_weights():
        for cd, out in ((core, wd), (1 - core, wd_send)):
            pick = picker(x, cd)
            own = mm(pick, wcat[...]).astype(BF16)
            for half in range(2):
                out[half, 0, 0:M] = own
                out[half, 1, 0:M] = mm(pick, w_next[half]).astype(BF16)
            for half in range(2):
                pick = picker(x_pair[1 - half], cd)
                out[half, 0, M : 2 * M] = mm(pick, wcat[...]).astype(BF16)
                out[half, 1, M : 2 * M] = mm(pick, w_next[half]).astype(BF16)

    tacc[...] = jnp.zeros_like(tacc)
    wacc[...] = jnp.zeros_like(wacc)
    woacc[...] = jnp.zeros_like(woacc)
    for r in range(R):
        gp[r, 0 : PAD - EDGE] = jnp.zeros((PAD - EDGE, LANES), F32)
        gp[r, NF + PAD + EDGE : NF + 2 * PAD] = jnp.zeros((PAD - EDGE, LANES), F32)

    def remote(src, dst, send, recv, device):
        return pltpu.make_async_remote_copy(
            src_ref=src,
            dst_ref=dst,
            send_sem=send,
            recv_sem=recv,
            device_id=device,
            device_id_type=MESH,
        )

    def edge_copies(kind):
        return (
            remote(
                halo_out.at[kind, 0],
                halo.at[kind, 0],
                halo_send.at[2 * kind],
                halo_recv.at[2 * kind],
                (up, t),
            ),
            remote(
                halo_out.at[kind, 1],
                halo.at[kind, 1],
                halo_send.at[2 * kind + 1],
                halo_recv.at[2 * kind + 1],
                (down, t),
            ),
        )

    def send_edges(kind, field):
        for r in range(R):
            halo_out[kind, 0, r] = field[r, PAD + NF - EDGE : PAD + NF]
            halo_out[kind, 1, r] = field[r, PAD : PAD + EDGE]
        for copy in edge_copies(kind):
            copy.start()

    def take_edges(kind, field):
        for copy in edge_copies(kind):
            copy.wait_recv()
        for r in range(R):
            field[r, PAD - EDGE : PAD] = jnp.where(s > 0, halo[kind, 0, r], 0.0)
            field[r, PAD + NF : PAD + NF + EDGE] = jnp.where(s < NS - 1, halo[kind, 1, r], 0.0)

    per_rec = NF // TM

    def forward(i, carry):
        r = lax.div(i, per_rec)
        part = lax.rem(i, per_rec)
        row0 = pl.multiple_of(part * TM, TM)
        rows = pl.ds(row0, TM)

        @pl.when(part == 0)
        def _():
            normed_load(r).wait()
            grads_load(r).start()

        both = mm(nv[r, rows, :], wcat[...])
        gate = jax.nn.sigmoid(both[:, LANES:])
        unit = both[:, :LANES] * gate
        gp[r, pl.ds(row0 + PAD, TM)] = jnp.where(valid(r, row0, TM), unit, 0.0)
        gs[r, rows] = gate
        a2[r, rows] = unit * (1.0 - gate)
        return carry

    lax.fori_loop(0, R * per_rec, forward, 0)
    pl.semaphore_wait(barrier, NS - 1 + 3)
    send_edges(0, gp)
    next_weights = [
        remote(wcat, w_next.at[half], wn_send.at[half], wn_recv.at[half], (s, pair[half]))
        for half in range(2)
    ]
    for copy in next_weights:
        copy.start()
    weight_swap = remote(wd_send, wd_oth, wx_send, wx_recv, (s, other))

    tap_rows = [taps[k : k + 1, :] for k in range(K)]
    tiles = NF // TC
    zero = jnp.zeros((8, LANES), F32)

    def conv_at(r, start, rows):
        total = tap_rows[0] * gp[r, pl.ds(start + PAD - H, rows)]
        for k in range(1, K):
            total = total + tap_rows[k] * gp[r, pl.ds(start + PAD - H + k, rows)]
        return total

    def conv_tile(r, i, sums):
        row0 = pl.multiple_of(i * TC, TC)
        total = conv_at(r, row0, TC)
        cv[r, pl.ds(row0 + PAD, TC)] = total
        kept = jnp.where(valid(r, row0, TC), total, 0.0)
        return sums[0] + fold(kept), sums[1] + fold(kept * kept)

    def conv_inner(r, sums):
        return lax.fori_loop(1, tiles - 1, functools.partial(conv_tile, r), sums)

    sums = lax.fori_loop(0, R, conv_inner, (zero, zero))
    loads[2].wait()

    def back_one(i, carry):
        r = lax.div(i, per_rec)
        part = lax.rem(i, per_rec)
        row0 = pl.multiple_of(part * TM, TM)

        @pl.when(part == 0)
        def _():
            grads_load(r).wait()

        both = mm(gv[r, pl.ds(row0, TM), :], wo[...])
        gn[r, pl.ds(row0 + PAD, TM)] = both[:, :LANES]
        feats[r, pl.ds(row0, TM)] = both[:, LANES:].astype(BF16)
        return carry

    lax.fori_loop(0, per_rec, back_one, 0)
    take_edges(0, gp)

    def conv_outer(r, sums):
        sums = conv_tile(r, 0, sums)
        return conv_tile(r, tiles - 1, sums)

    sums = lax.fori_loop(0, R, conv_outer, sums)

    def red_wait(red, index):
        part = red.at[pl.ds(0, NS - 1)]
        pltpu.make_async_copy(part, part, red_recv.at[index]).wait()

    def red_sent(red, index):
        part = red.at[pl.ds(0, NS - 1)]
        pltpu.make_async_copy(part, part, red_send.at[index]).wait()

    def spread_from(red, index):
        def give(k, carry):
            remote(
                red.at[s], red.at[s], red_send.at[index], red_recv.at[index], (lax.rem(s + k, NS), t)
            ).start()
            return carry

        lax.fori_loop(1, NS, give, 0)

    def spread(red, index, value):
        red[s] = value
        spread_from(red, index)

    def two_rows(first, second):
        row = lax.broadcasted_iota(jnp.int32, (8, LANES), 0)
        first = jnp.sum(first, axis=0, keepdims=True)
        second = jnp.sum(second, axis=0, keepdims=True)
        return jnp.where(row == 0, first, jnp.where(row == 1, second, 0.0))

    def collect(red, index):
        red_wait(red, index)
        total = red[0]
        for k in range(1, NS):
            total = total + red[k]
        return total

    spread(red_a, 0, two_rows(*sums))

    for r in range(R):
        cv[r, PAD - EDGE : PAD] = conv_at(r, -EDGE, EDGE)
        cv[r, PAD + NF : PAD + NF + EDGE] = conv_at(r, NF, EDGE)
    def chunk_place(q):
        r = lax.div(q, cpr)
        return r, pl.multiple_of(lax.rem(q, cpr) * F, F)

    lax.fori_loop(per_rec, R * per_rec, back_one, 0)

    total = collect(red_a, 0)
    count = (lengths[0] + lengths[1] + lengths[2] + lengths[3]).astype(F32)
    inv_count = 1.0 / jnp.full((1, LANES), count, F32)
    centre = total[0:1] * inv_count
    spread_sq = total[1:2] * inv_count - centre * centre
    inv_std = lax.rsqrt(spread_sq + EPS)
    gain_row = gain[...]
    shift_row = shift[...]

    def norm_rec(r, sums):
        def norm_tile(i, sums):
            row0 = pl.multiple_of(i * TC, TC)
            rows = pl.ds(row0, TC)
            padded = pl.ds(row0 + PAD, TC)
            unit = (cv[r, padded] - centre) * inv_std
            normalized = unit * gain_row + shift_row
            sig = jax.nn.sigmoid(normalized)
            ok = valid(r, row0, TC)
            sw[r, rows] = jnp.where(ok, normalized * sig, 0.0).astype(BF16)
            grad = gn[r, padded] * sig * (1.0 + normalized * (1.0 - sig))
            grad = jnp.where(ok, grad, 0.0)
            gn[r, padded] = grad
            return sums[0] + fold(grad), sums[1] + fold(grad * unit)

        return lax.fori_loop(0, tiles, norm_tile, sums)

    sums = lax.fori_loop(0, R, norm_rec, (zero, zero))
    spread(red_b, 1, two_rows(*sums))
    send_edges(1, gn)

    def out_weight_part(q, carry):
        r, row0 = chunk_place(q)
        rows = pl.ds(row0, F)
        woacc[...] += mm_tl(sw[r, rows, :], gv[r, rows, :])
        return carry

    lax.fori_loop(0, NCH, out_weight_part, 0)

    def turn_weight(index, acc, first):
        for b in range(D // LANES):
            wsend[index, b * LANES : (b + 1) * LANES, :] = jnp.transpose(
                acc[first : first + LANES, b * LANES : (b + 1) * LANES]
            )

    def ship_weight(index):
        def give(k, carry):
            p = lax.rem(s + k, NS)
            remote(
                wsend.at[index, pl.ds(pl.multiple_of(p * DP, DP), DP)],
                wrecv.at[index, s],
                wr_send.at[index],
                wr_recv.at[index],
                (p, t),
            ).start()
            return carry

        lax.fori_loop(1, NS, give, 0)
        wrecv[index, s] = wsend[index, pl.ds(pl.multiple_of(s * DP, DP), DP)]

    turn_weight(2, woacc, 0)
    for copy in next_weights:
        copy.wait_recv()
    pick_weights()
    weight_swap.start()
    total = collect(red_b, 1)
    ship_weight(2)
    gshift[...] = total[0:1]
    ggain[...] = total[1:2]
    scale = gain_row * inv_std
    mean_shift = total[0:1] * inv_count
    mean_gain = total[1:2] * inv_count

    take_edges(1, gn)
    padded_rows = NF + 2 * EDGE
    TE = padded_rows // 10 if padded_rows % 80 == 0 else 8

    def conv_grad(r):
        def conv_grad_tile(i, carry):
            row0 = pl.multiple_of(i * TE, TE)
            rows = pl.ds(row0 + PAD - EDGE, TE)
            unit = (cv[r, rows] - centre) * inv_std
            grad = scale * (gn[r, rows] - mean_shift - unit * mean_gain)
            gc[r, rows] = jnp.where(valid(r, row0 - EDGE, TE), grad, 0.0)
            return carry

        lax.fori_loop(0, padded_rows // TE, conv_grad_tile, 0)

    def swap_copy(q, group):
        return remote(
            gmine.at[q, group],
            gother.at[q, group],
            ge_send,
            ge_recv.at[2 * q + group],
            (s, other),
        )

    def turn_of(i):
        half = lax.rem(i, 2)
        return half, half * (NCH // 2) + lax.div(i, 2)

    def pair_copy(half, q):
        to = pair[0] * (1 - half) + pair[1] * half
        return remote(gg_out.at[q], gg_in.at[q], gg_send, gg_recv.at[q], (s, to))

    def far_copy(half, q):
        to = pair[1] * (1 - half) + pair[0] * half
        return remote(far_out.at[q], far_in.at[q], fr_send, fr_recv.at[q], (s, to))

    def pointwise_grads(q):
        r, base = chunk_place(q)

        def tile(i, taps_sum):
            row0 = pl.multiple_of(base + i * TC, TC)
            rows = pl.ds(row0, TC)
            here = pl.ds(pl.multiple_of(i * TC, TC), TC)
            grad = tap_rows[0] * gc[r, pl.ds(row0 + PAD + H, TC)]
            for k in range(1, K):
                grad = grad + tap_rows[k] * gc[r, pl.ds(row0 + PAD + H - k, TC)]
            grad = jnp.where(valid(r, row0, TC), grad, 0.0)
            gg_out[q, here] = grad.astype(BF16)
            gmine[q, 0, here, 0:LANES] = (grad * gs[r, rows]).astype(BF16)
            gmine[q, 0, here, LANES : 2 * LANES] = (grad * a2[r, rows]).astype(BF16)
            centre_rows = gc[r, pl.ds(row0 + PAD, TC)]
            return tuple(
                taps_sum[k] + fold(centre_rows * gp[r, pl.ds(row0 + PAD - H + k, TC)])
                for k in range(K)
            )

        taps_sum = lax.fori_loop(0, F // TC, tile, tuple(tacc[k] for k in range(K)))
        for k in range(K):
            tacc[k] = taps_sum[k]

    def pair_grads(half, q):
        r, row0 = chunk_place(q)
        both = mm(nv[r, pl.ds(row0, F), :], w_next[half])
        gate = jax.nn.sigmoid(both[:, LANES:])
        unit = both[:, :LANES] * gate
        pair_copy(half, q).wait_recv()
        grad = gg_in[q].astype(F32)
        gmine[q, 1, :, 0:LANES] = (grad * gate).astype(BF16)
        gmine[q, 1, :, LANES : 2 * LANES] = (grad * (unit * (1.0 - gate))).astype(BF16)
        swap_copy(q, 1).start()

    row = lax.broadcasted_iota(jnp.int32, (M, LANES), 0)
    col = lax.broadcasted_iota(jnp.int32, (M, LANES), 1)
    own_rows = jnp.where(row == col, 1.0, 0.0).astype(BF16)

    def far_sends(half, q):
        r, row0 = chunk_place(q)
        total = mm_t(wd[half, 0], gmine[q, 0]) + mm_t(wd[half, 1], gmine[q, 1])
        for group in range(2):
            swap_copy(q, group).wait_recv()
        total = total + (mm_t(wd_oth[half, 0], gother[q, 0]) + mm_t(wd_oth[half, 1], gother[q, 1]))
        far_out[q] = total[M:].astype(BF16)
        far_copy(half, q).start()
        own_part[q] = total[:M] + mm_t(own_rows, feats[r, pl.ds(row0, F)])

    def out_place(q, owner):
        r, row0 = chunk_place(q)
        return gin.at[r, :, pl.ds(pl.multiple_of(owner * NF + row0, F), F)]

    def own_copy(q):
        return pltpu.make_async_copy(osend.at[q, s], out_place(q, s), aa_own.at[q])

    def finish(half, q):
        far_copy(half, q).wait_recv()
        total = own_part[q] + far_in[q].astype(F32)
        osend[q] = total.astype(BF16).reshape(NS, 8, F)

        def give(k, carry):
            p = lax.rem(s + k, NS)
            remote(osend.at[q, p], out_place(q, s), aa_send, aa_recv, (p, t)).start()
            return carry

        lax.fori_loop(1, NS, give, 0)
        own_copy(q).start()

    def weight_part(q):
        r, row0 = chunk_place(q)
        wacc[...] += mm_tl(gmine[q, 0], nv[r, pl.ds(row0, F), :])

    for k in range(K, 16):
        red_c[s, k : k + 1] = jnp.zeros((1, LANES), F32)

    def outward(i, carry):
        half, q = turn_of(i)

        @pl.when(lax.rem(q, cpr) == 0)
        def _():
            conv_grad(lax.div(q, cpr))

        pointwise_grads(q)
        pair_copy(half, q).start()
        swap_copy(q, 0).start()
        weight_part(q)
        return carry

    lax.fori_loop(0, NCH, outward, 0)
    for index in range(2):
        turn_weight(index, wacc, index * LANES)
        ship_weight(index)
    for k in range(K):
        red_c[s, k : k + 1] = jnp.sum(tacc[k], axis=0, keepdims=True)
    spread_from(red_c, 2)
    weight_swap.wait_recv()
    LAG_B, LAG_C = 1, 4

    def homeward(i, carry):
        @pl.when(i < NCH)
        def _():
            pair_grads(*turn_of(i))

        @pl.when(i == NCH)
        def _():
            gtaps[...] = collect(red_c, 2)[0:K]

            for index, out in ((2, gwo), (0, gwv), (1, gwg)):
                slots = wrecv.at[index, pl.ds(0, NS - 1)]
                pltpu.make_async_copy(slots, slots, wr_recv.at[index]).wait()
                total = wrecv[index, 0]
                for k in range(1, NS):
                    total = total + wrecv[index, k]
                out[...] = total

        @pl.when(jnp.logical_and(i >= LAG_B, i < NCH + LAG_B))
        def _():
            far_sends(*turn_of(i - LAG_B))

        @pl.when(i >= LAG_C)
        def _():
            finish(*turn_of(i - LAG_C))

        return carry

    lax.fori_loop(0, NCH + LAG_C, homeward, 0)

    for copy in next_weights:
        copy.wait_send()
    weight_swap.wait_send()
    for kind in range(2):
        for copy in edge_copies(kind):
            copy.wait_send()
    red_sent(red_a, 0)
    red_sent(red_b, 1)
    red_sent(red_c, 2)
    for index in range(3):
        slots = wrecv.at[index, pl.ds(0, NS - 1)]
        pltpu.make_async_copy(slots, slots, wr_send.at[index]).wait()

    def sent(whole, semaphore):
        pltpu.make_async_copy(whole, whole, semaphore).wait()

    sent(gmine, ge_send)
    sent(gg_out, gg_send)
    sent(far_out, fr_send)
    for q in range(NCH):
        own_copy(q).wait()
    others = osend.at[:, pl.ds(0, NS - 1)]
    sent(others, aa_send)
    sent(others, aa_recv)


def hand_on(*refs):
    half = (len(refs) - 1) // 2
    sems = refs[-1]
    copies = [pltpu.make_async_copy(refs[i], refs[half + i], sems.at[i]) for i in range(half)]
    for copy in copies:
        copy.start()
    for copy in copies:
        copy.wait()


def per_device(
    normed,
    grad_out,
    value_weight,
    gate_weight,
    depth_taps,
    norm_gain,
    norm_shift,
    out_weight,
    lengths,
):
    R, NF, D = normed.shape
    K, CW = depth_taps.shape
    NS = lax.axis_size("seq")
    M = 8 * NS
    F = min(512, NF)
    TM = min(512, NF)
    TC = min(64, F)
    NCH = R * NF // F
    DP = D // NS
    cfg = (R, NF, D, NS, F, TM, TC)
    vmem = pl.BlockSpec(memory_space=pltpu.VMEM)
    hbm = pl.BlockSpec(memory_space=pl.ANY)
    dma = pltpu.SemaphoreType.DMA
    padded = NF + 2 * PAD
    out_shape = (
        jax.ShapeDtypeStruct((R, 8, NS * NF), BF16),
        jax.ShapeDtypeStruct((DP, CW), F32),
        jax.ShapeDtypeStruct((DP, CW), F32),
        jax.ShapeDtypeStruct((DP, CW), F32),
        jax.ShapeDtypeStruct((K, CW), F32),
        jax.ShapeDtypeStruct((1, CW), F32),
        jax.ShapeDtypeStruct((1, CW), F32),
    )
    scratch = [
        pltpu.VMEM((R, NF, D), BF16),
        pltpu.VMEM((R, NF, D), BF16),
        pltpu.VMEM((D, 2 * LANES), BF16),
        pltpu.VMEM((D, 2 * LANES), BF16),
        pltpu.VMEM((2, D, 2 * LANES), BF16),
        pltpu.VMEM((2, 2, 2 * M, 2 * LANES), BF16),
        pltpu.VMEM((2, 2, 2 * M, 2 * LANES), BF16),
        pltpu.VMEM((2, 2, 2 * M, 2 * LANES), BF16),
        pltpu.VMEM((R, NF, LANES), BF16),
        pltpu.VMEM((NCH, M, F), F32),
        pltpu.VMEM((R, padded, LANES), F32),
        pltpu.VMEM((R, NF, LANES), F32),
        pltpu.VMEM((R, NF, LANES), F32),
        pltpu.VMEM((R, padded, LANES), F32),
        pltpu.VMEM((R, padded, LANES), F32),
        pltpu.VMEM((R, padded, LANES), F32),
        pltpu.VMEM((R, NF, LANES), BF16),
        pltpu.VMEM((2, 2, R, EDGE, LANES), F32),
        pltpu.VMEM((2, 2, R, EDGE, LANES), F32),
        pltpu.VMEM((NS, 8, LANES), F32),
        pltpu.VMEM((NS, 8, LANES), F32),
        pltpu.VMEM((NS, 16, LANES), F32),
        pltpu.VMEM((NCH, F, LANES), BF16),
        pltpu.VMEM((NCH, F, LANES), BF16),
        pltpu.VMEM((NCH, 2, F, 2 * LANES), BF16),
        pltpu.VMEM((NCH, 2, F, 2 * LANES), BF16),
        pltpu.VMEM((NCH, M, F), BF16),
        pltpu.VMEM((NCH, M, F), BF16),
        pltpu.VMEM((NCH, NS, 8, F), BF16),
        pltpu.VMEM((K, 8, LANES), F32),
        pltpu.VMEM((2 * LANES, D), F32),
        pltpu.VMEM((LANES, D), F32),
        pltpu.VMEM((3, D, LANES), F32),
        pltpu.VMEM((3, NS, DP, LANES), F32),
        dma((3 + 2 * R,)),
        dma((4,)),
        dma((4,)),
        dma((3,)),
        dma((3,)),
        dma,
        dma,
        dma((2,)),
        dma((2,)),
        dma,
        dma((2 * NCH,)),
        dma,
        dma((NCH,)),
        dma,
        dma((NCH,)),
        dma,
        dma,
        dma((NCH,)),
        dma((3,)),
        dma((3,)),
    ]
    outs = pl.pallas_call(
        functools.partial(kernel, cfg),
        out_shape=tuple(pltpu.VMEM(o.shape, o.dtype) for o in out_shape),
        in_specs=[pl.BlockSpec(memory_space=pltpu.SMEM)] + [hbm] * 5 + [vmem] * 3,
        out_specs=(vmem,) * 7,
        scratch_shapes=scratch,
        compiler_params=pltpu.CompilerParams(
            collective_id=0, has_side_effects=True, vmem_limit_bytes=60 * 1024 * 1024
        ),
        cost_estimate=pl.CostEstimate(
            flops=8 * 2 * R * NF * D * CW, bytes_accessed=4 * R * NF * D, transcendentals=0
        ),
    )(
        lengths,
        normed,
        grad_out,
        value_weight,
        gate_weight,
        out_weight,
        depth_taps,
        norm_gain.reshape(1, CW),
        norm_shift.reshape(1, CW),
    )
    held = [pltpu.with_memory_space_constraint(o, pltpu.VMEM) for o in outs]
    moved = pl.pallas_call(
        hand_on,
        out_shape=out_shape,
        in_specs=[vmem] * len(out_shape),
        out_specs=(hbm,) * len(out_shape),
        scratch_shapes=[dma((len(out_shape),))],
    )(*held)
    grad_in, grad_wv, grad_wg, grad_wo, grad_taps, grad_gain, grad_shift = moved
    return (
        grad_in,
        grad_wv,
        grad_wg,
        grad_wo,
        grad_taps,
        grad_gain.reshape(CW),
        grad_shift.reshape(CW),
    )


def solution(mesh):
    placed = (
        P(None, "seq", None),
        P(None, "seq", None),
        P(None, "tp"),
        P(None, "tp"),
        P(None, "tp"),
        P("tp"),
        P("tp"),
        P(None, "tp"),
        P(),
    )
    return jax.shard_map(
        per_device,
        mesh=mesh,
        in_specs=placed,
        out_specs=(
            P(None, ("seq", "tp"), None),
            P("seq", "tp"),
            P("seq", "tp"),
            P("seq", "tp"),
            P(None, "tp"),
            P("tp"),
            P("tp"),
        ),
        check_vma=False,
    )
```

```python
import functools

import jax
import jax.numpy as jnp
from jax import lax
from jax.experimental import pallas as pl
from jax.experimental.pallas import tpu as pltpu
from jax.sharding import PartitionSpec as P

MESH = pl.DeviceIdType.MESH
F32 = jnp.float32
BF16 = jnp.bfloat16
EPS = 1e-05
LANES = 128
EDGE = 8
PAD = 16
XN = 4


def mm(a, b):
    return jnp.dot(a, b, preferred_element_type=F32)


def mm_t(a, b):
    return lax.dot_general(a, b, (((1,), (1,)), ((), ())), preferred_element_type=F32)


def mm_tl(a, b):
    return lax.dot_general(a, b, (((0,), (0,)), ((), ())), preferred_element_type=F32)


def fold(v):
    rows = v.shape[0]
    return jnp.sum(v.reshape(rows // 8, 8, LANES), axis=0)


def kernel(
    cfg,
    lengths,
    normed_h,
    grads_h,
    wv_h,
    wg_h,
    wo_h,
    taps,
    gain,
    shift,
    gin,
    gwv,
    gwg,
    gwo,
    gtaps,
    ggain,
    gshift,
    nv,
    gv,
    wcat,
    wo,
    w_next,
    wd,
    wd_send,
    wd_oth,
    feats,
    own_part,
    gp,
    gs,
    a2,
    cv,
    gn,
    gc,
    sw,
    halo_out,
    halo,
    red_a,
    red_b,
    red_c,
    gg_out,
    gg_in,
    gmine,
    gother,
    far_out,
    far_in,
    osend,
    tacc,
    wacc,
    woacc,
    wsend,
    wrecv,
    load_sem,
    halo_send,
    halo_recv,
    red_send,
    red_recv,
    wx_send,
    wx_recv,
    wn_send,
    wn_recv,
    ge_send,
    ge_recv,
    gg_send,
    gg_recv,
    fr_send,
    fr_recv,
    aa_send,
    aa_recv,
    aa_own,
    wr_send,
    wr_recv,
):
    R, NF, D, NS, F, TM, TC = cfg
    K = taps.shape[0]
    H = (K - 1) // 2
    M = 8 * NS
    NCH = R * NF // F
    cpr = NF // F
    DP = D // NS
    s = lax.axis_index("seq")
    t = lax.axis_index("tp")
    x = lax.div(t, 2)
    core = lax.rem(t, 2)
    other = x * 2 + (1 - core)
    step = 1 - 2 * lax.rem(x, 2)
    x_pair = (x + step, lax.rem(x + XN - step, XN))
    pair = tuple(xp * 2 + core for xp in x_pair)
    up = lax.rem(s + 1, NS)
    down = lax.rem(s + NS - 1, NS)

    barrier = pltpu.get_barrier_semaphore()

    def greet(k, carry):
        pl.semaphore_signal(
            barrier, inc=1, device_id=(lax.rem(s + k, NS), t), device_id_type=MESH
        )
        return carry

    lax.fori_loop(1, NS, greet, 0)
    for mate in (other,) + pair:
        pl.semaphore_signal(barrier, inc=1, device_id=(s, mate), device_id_type=MESH)

    loads = [
        pltpu.make_async_copy(wv_h, wcat.at[:, 0:LANES], load_sem.at[0]),
        pltpu.make_async_copy(wg_h, wcat.at[:, LANES : 2 * LANES], load_sem.at[1]),
        pltpu.make_async_copy(wo_h, wo.at[:, 0:LANES], load_sem.at[2]),
    ]
    for load in loads:
        load.start()

    def normed_load(r):
        return pltpu.make_async_copy(normed_h.at[r], nv.at[r], load_sem.at[3 + r])

    def grads_load(r):
        return pltpu.make_async_copy(grads_h.at[r], gv.at[r], load_sem.at[3 + R + r])

    for r in range(R):
        normed_load(r).start()

    def valid(r, row0, rows):
        at = s * NF + row0 + lax.broadcasted_iota(jnp.int32, (rows, LANES), 0)
        return jnp.logical_and(at >= 0, at < lengths[r])

    def picker(xd, cd):
        row = lax.broadcasted_iota(jnp.int32, (M, D), 0)
        col = lax.broadcasted_iota(jnp.int32, (M, D), 1)
        want = (row // 8) * 64 + xd * 16 + cd * 8 + row % 8
        return jnp.where(col == want, 1.0, 0.0).astype(BF16)

    feature = lax.broadcasted_iota(jnp.int32, (D, LANES), 0)
    place = lax.broadcasted_iota(jnp.int32, (D, LANES), 1)
    want = (place // 8) * 64 + x * 16 + core * 8 + place % 8
    wo[:, LANES : 2 * LANES] = jnp.where(
        jnp.logical_and(feature == want, place < M), 1.0, 0.0
    ).astype(BF16)
    loads[0].wait()
    loads[1].wait()

    def pick_weights():
        for cd, out in ((core, wd), (1 - core, wd_send)):
            pick = picker(x, cd)
            own = mm(pick, wcat[...]).astype(BF16)
            for half in range(2):
                out[half, 0, 0:M] = own
                out[half, 1, 0:M] = mm(pick, w_next[half]).astype(BF16)
            for half in range(2):
                pick = picker(x_pair[1 - half], cd)
                out[half, 0, M : 2 * M] = mm(pick, wcat[...]).astype(BF16)
                out[half, 1, M : 2 * M] = mm(pick, w_next[half]).astype(BF16)

    tacc[...] = jnp.zeros_like(tacc)
    wacc[...] = jnp.zeros_like(wacc)
    woacc[...] = jnp.zeros_like(woacc)
    for r in range(R):
        gp[r, 0 : PAD - EDGE] = jnp.zeros((PAD - EDGE, LANES), F32)
        gp[r, NF + PAD + EDGE : NF + 2 * PAD] = jnp.zeros((PAD - EDGE, LANES), F32)

    def remote(src, dst, send, recv, device):
        return pltpu.make_async_remote_copy(
            src_ref=src,
            dst_ref=dst,
            send_sem=send,
            recv_sem=recv,
            device_id=device,
            device_id_type=MESH,
        )

    def edge_copies(kind):
        return (
            remote(
                halo_out.at[kind, 0],
                halo.at[kind, 0],
                halo_send.at[2 * kind],
                halo_recv.at[2 * kind],
                (up, t),
            ),
            remote(
                halo_out.at[kind, 1],
                halo.at[kind, 1],
                halo_send.at[2 * kind + 1],
                halo_recv.at[2 * kind + 1],
                (down, t),
            ),
        )

    def send_edges(kind, field):
        for r in range(R):
            halo_out[kind, 0, r] = field[r, PAD + NF - EDGE : PAD + NF]
            halo_out[kind, 1, r] = field[r, PAD : PAD + EDGE]
        for copy in edge_copies(kind):
            copy.start()

    def take_edges(kind, field):
        for copy in edge_copies(kind):
            copy.wait_recv()
        for r in range(R):
            field[r, PAD - EDGE : PAD] = jnp.where(s > 0, halo[kind, 0, r], 0.0)
            field[r, PAD + NF : PAD + NF + EDGE] = jnp.where(s < NS - 1, halo[kind, 1, r], 0.0)

    per_rec = NF // TM

    def forward(i, carry):
        r = lax.div(i, per_rec)
        part = lax.rem(i, per_rec)
        row0 = pl.multiple_of(part * TM, TM)
        rows = pl.ds(row0, TM)

        @pl.when(part == 0)
        def _():
            normed_load(r).wait()
            grads_load(r).start()

        both = mm(nv[r, rows, :], wcat[...])
        gate = jax.nn.sigmoid(both[:, LANES:])
        unit = both[:, :LANES] * gate
        gp[r, pl.ds(row0 + PAD, TM)] = jnp.where(valid(r, row0, TM), unit, 0.0)
        gs[r, rows] = gate
        a2[r, rows] = unit * (1.0 - gate)
        return carry

    lax.fori_loop(0, R * per_rec, forward, 0)
    pl.semaphore_wait(barrier, NS - 1 + 3)
    send_edges(0, gp)
    next_weights = [
        remote(wcat, w_next.at[half], wn_send.at[half], wn_recv.at[half], (s, pair[half]))
        for half in range(2)
    ]
    for copy in next_weights:
        copy.start()
    weight_swap = remote(wd_send, wd_oth, wx_send, wx_recv, (s, other))

    tap_rows = [taps[k : k + 1, :] for k in range(K)]
    tiles = NF // TC
    zero = jnp.zeros((8, LANES), F32)

    def conv_at(r, start, rows):
        total = tap_rows[0] * gp[r, pl.ds(start + PAD - H, rows)]
        for k in range(1, K):
            total = total + tap_rows[k] * gp[r, pl.ds(start + PAD - H + k, rows)]
        return total

    def conv_tile(r, i, sums):
        row0 = pl.multiple_of(i * TC, TC)
        total = conv_at(r, row0, TC)
        cv[r, pl.ds(row0 + PAD, TC)] = total
        kept = jnp.where(valid(r, row0, TC), total, 0.0)
        return sums[0] + fold(kept), sums[1] + fold(kept * kept)

    def conv_inner(r, sums):
        return lax.fori_loop(1, tiles - 1, functools.partial(conv_tile, r), sums)

    sums = lax.fori_loop(0, R, conv_inner, (zero, zero))
    loads[2].wait()

    def back_one(i, carry):
        r = lax.div(i, per_rec)
        part = lax.rem(i, per_rec)
        row0 = pl.multiple_of(part * TM, TM)

        @pl.when(part == 0)
        def _():
            grads_load(r).wait()

        both = mm(gv[r, pl.ds(row0, TM), :], wo[...])
        gn[r, pl.ds(row0 + PAD, TM)] = both[:, :LANES]
        feats[r, pl.ds(row0, TM)] = both[:, LANES:].astype(BF16)
        return carry

    lax.fori_loop(0, per_rec, back_one, 0)
    take_edges(0, gp)

    def conv_outer(r, sums):
        sums = conv_tile(r, 0, sums)
        return conv_tile(r, tiles - 1, sums)

    sums = lax.fori_loop(0, R, conv_outer, sums)

    def red_wait(red, index):
        part = red.at[pl.ds(0, NS - 1)]
        pltpu.make_async_copy(part, part, red_recv.at[index]).wait()

    def red_sent(red, index):
        part = red.at[pl.ds(0, NS - 1)]
        pltpu.make_async_copy(part, part, red_send.at[index]).wait()

    def spread_from(red, index):
        def give(k, carry):
            remote(
                red.at[s], red.at[s], red_send.at[index], red_recv.at[index], (lax.rem(s + k, NS), t)
            ).start()
            return carry

        lax.fori_loop(1, NS, give, 0)

    def spread(red, index, value):
        red[s] = value
        spread_from(red, index)

    def two_rows(first, second):
        row = lax.broadcasted_iota(jnp.int32, (8, LANES), 0)
        first = jnp.sum(first, axis=0, keepdims=True)
        second = jnp.sum(second, axis=0, keepdims=True)
        return jnp.where(row == 0, first, jnp.where(row == 1, second, 0.0))

    def collect(red, index):
        red_wait(red, index)
        total = red[0]
        for k in range(1, NS):
            total = total + red[k]
        return total

    spread(red_a, 0, two_rows(*sums))

    for r in range(R):
        cv[r, PAD - EDGE : PAD] = conv_at(r, -EDGE, EDGE)
        cv[r, PAD + NF : PAD + NF + EDGE] = conv_at(r, NF, EDGE)
    def chunk_place(q):
        r = lax.div(q, cpr)
        return r, pl.multiple_of(lax.rem(q, cpr) * F, F)

    lax.fori_loop(per_rec, R * per_rec, back_one, 0)

    total = collect(red_a, 0)
    count = (lengths[0] + lengths[1] + lengths[2] + lengths[3]).astype(F32)
    inv_count = 1.0 / jnp.full((1, LANES), count, F32)
    centre = total[0:1] * inv_count
    spread_sq = total[1:2] * inv_count - centre * centre
    inv_std = lax.rsqrt(spread_sq + EPS)
    gain_row = gain[...]
    shift_row = shift[...]

    def norm_rec(r, sums):
        def norm_tile(i, sums):
            row0 = pl.multiple_of(i * TC, TC)
            rows = pl.ds(row0, TC)
            padded = pl.ds(row0 + PAD, TC)
            unit = (cv[r, padded] - centre) * inv_std
            normalized = unit * gain_row + shift_row
            sig = jax.nn.sigmoid(normalized)
            ok = valid(r, row0, TC)
            sw[r, rows] = jnp.where(ok, normalized * sig, 0.0).astype(BF16)
            grad = gn[r, padded] * sig * (1.0 + normalized * (1.0 - sig))
            grad = jnp.where(ok, grad, 0.0)
            gn[r, padded] = grad
            return sums[0] + fold(grad), sums[1] + fold(grad * unit)

        return lax.fori_loop(0, tiles, norm_tile, sums)

    sums = lax.fori_loop(0, R, norm_rec, (zero, zero))
    spread(red_b, 1, two_rows(*sums))
    send_edges(1, gn)

    def out_weight_part(q, carry):
        r, row0 = chunk_place(q)
        rows = pl.ds(row0, F)
        woacc[...] += mm_tl(sw[r, rows, :], gv[r, rows, :])
        return carry

    lax.fori_loop(0, NCH, out_weight_part, 0)

    def turn_weight(index, acc, first):
        for b in range(D // LANES):
            wsend[index, b * LANES : (b + 1) * LANES, :] = jnp.transpose(
                acc[first : first + LANES, b * LANES : (b + 1) * LANES]
            ).astype(BF16)

    def ship_weight(index):
        def give(k, carry):
            p = lax.rem(s + k, NS)
            remote(
                wsend.at[index, pl.ds(pl.multiple_of(p * DP, DP), DP)],
                wrecv.at[index, s],
                wr_send.at[index],
                wr_recv.at[index],
                (p, t),
            ).start()
            return carry

        lax.fori_loop(1, NS, give, 0)
        wrecv[index, s] = wsend[index, pl.ds(pl.multiple_of(s * DP, DP), DP)]

    turn_weight(2, woacc, 0)
    for copy in next_weights:
        copy.wait_recv()
    pick_weights()
    weight_swap.start()
    total = collect(red_b, 1)
    ship_weight(2)
    gshift[...] = total[0:1]
    ggain[...] = total[1:2]
    scale = gain_row * inv_std
    mean_shift = total[0:1] * inv_count
    mean_gain = total[1:2] * inv_count

    take_edges(1, gn)
    padded_rows = NF + 2 * EDGE
    TE = padded_rows // 10 if padded_rows % 80 == 0 else 8

    def conv_grad(r):
        def conv_grad_tile(i, carry):
            row0 = pl.multiple_of(i * TE, TE)
            rows = pl.ds(row0 + PAD - EDGE, TE)
            unit = (cv[r, rows] - centre) * inv_std
            grad = scale * (gn[r, rows] - mean_shift - unit * mean_gain)
            gc[r, rows] = jnp.where(valid(r, row0 - EDGE, TE), grad, 0.0)
            return carry

        lax.fori_loop(0, padded_rows // TE, conv_grad_tile, 0)

    def swap_copy(q, group):
        return remote(
            gmine.at[q, group],
            gother.at[q, group],
            ge_send,
            ge_recv.at[2 * q + group],
            (s, other),
        )

    def turn_of(i):
        half = lax.rem(i, 2)
        return half, half * (NCH // 2) + lax.div(i, 2)

    def pair_copy(half, q):
        to = pair[0] * (1 - half) + pair[1] * half
        return remote(gg_out.at[q], gg_in.at[q], gg_send, gg_recv.at[q], (s, to))

    def far_copy(half, q):
        to = pair[1] * (1 - half) + pair[0] * half
        return remote(far_out.at[q], far_in.at[q], fr_send, fr_recv.at[q], (s, to))

    def pointwise_grads(q):
        r, base = chunk_place(q)

        def tile(i, taps_sum):
            row0 = pl.multiple_of(base + i * TC, TC)
            rows = pl.ds(row0, TC)
            here = pl.ds(pl.multiple_of(i * TC, TC), TC)
            grad = tap_rows[0] * gc[r, pl.ds(row0 + PAD + H, TC)]
            for k in range(1, K):
                grad = grad + tap_rows[k] * gc[r, pl.ds(row0 + PAD + H - k, TC)]
            grad = jnp.where(valid(r, row0, TC), grad, 0.0)
            gg_out[q, here] = grad.astype(BF16)
            gmine[q, 0, here, 0:LANES] = (grad * gs[r, rows]).astype(BF16)
            gmine[q, 0, here, LANES : 2 * LANES] = (grad * a2[r, rows]).astype(BF16)
            centre_rows = gc[r, pl.ds(row0 + PAD, TC)]
            return tuple(
                taps_sum[k] + fold(centre_rows * gp[r, pl.ds(row0 + PAD - H + k, TC)])
                for k in range(K)
            )

        taps_sum = lax.fori_loop(0, F // TC, tile, tuple(tacc[k] for k in range(K)))
        for k in range(K):
            tacc[k] = taps_sum[k]

    def pair_grads(half, q):
        r, row0 = chunk_place(q)
        both = mm(nv[r, pl.ds(row0, F), :], w_next[half])
        gate = jax.nn.sigmoid(both[:, LANES:])
        unit = both[:, :LANES] * gate
        pair_copy(half, q).wait_recv()
        grad = gg_in[q].astype(F32)
        gmine[q, 1, :, 0:LANES] = (grad * gate).astype(BF16)
        gmine[q, 1, :, LANES : 2 * LANES] = (grad * (unit * (1.0 - gate))).astype(BF16)
        swap_copy(q, 1).start()

    row = lax.broadcasted_iota(jnp.int32, (M, LANES), 0)
    col = lax.broadcasted_iota(jnp.int32, (M, LANES), 1)
    own_rows = jnp.where(row == col, 1.0, 0.0).astype(BF16)

    def far_sends(half, q):
        r, row0 = chunk_place(q)
        total = mm_t(wd[half, 0], gmine[q, 0]) + mm_t(wd[half, 1], gmine[q, 1])
        for group in range(2):
            swap_copy(q, group).wait_recv()
        total = total + (mm_t(wd_oth[half, 0], gother[q, 0]) + mm_t(wd_oth[half, 1], gother[q, 1]))
        far_out[q] = total[M:].astype(BF16)
        far_copy(half, q).start()
        own_part[q] = total[:M] + mm_t(own_rows, feats[r, pl.ds(row0, F)])

    def out_place(q, owner):
        r, row0 = chunk_place(q)
        return gin.at[r, :, pl.ds(pl.multiple_of(owner * NF + row0, F), F)]

    def own_copy(q):
        return pltpu.make_async_copy(osend.at[q, s], out_place(q, s), aa_own.at[q])

    def finish(half, q):
        far_copy(half, q).wait_recv()
        total = own_part[q] + far_in[q].astype(F32)
        osend[q] = total.astype(BF16).reshape(NS, 8, F)

        def give(k, carry):
            p = lax.rem(s + k, NS)
            remote(osend.at[q, p], out_place(q, s), aa_send, aa_recv, (p, t)).start()
            return carry

        lax.fori_loop(1, NS, give, 0)
        own_copy(q).start()

    def weight_part(q):
        r, row0 = chunk_place(q)
        wacc[...] += mm_tl(gmine[q, 0], nv[r, pl.ds(row0, F), :])

    for k in range(K, 16):
        red_c[s, k : k + 1] = jnp.zeros((1, LANES), F32)

    def outward(i, carry):
        half, q = turn_of(i)

        @pl.when(lax.rem(q, cpr) == 0)
        def _():
            conv_grad(lax.div(q, cpr))

        pointwise_grads(q)
        pair_copy(half, q).start()
        swap_copy(q, 0).start()

        @pl.when(i < NCH - 8)
        def _():
            weight_part(q)

        return carry

    lax.fori_loop(0, NCH, outward, 0)
    weight_swap.wait_recv()
    LAG_B, LAG_C = 1, 4

    def homeward(i, carry):
        @pl.when(i < NCH)
        def _():
            pair_grads(*turn_of(i))

        @pl.when(i < 2)
        def _():
            for k in range(4):
                weight_part(turn_of(NCH - 8 + 4 * i + k)[1])

        @pl.when(i == 1)
        def _():
            for index in range(2):
                turn_weight(index, wacc, index * LANES)
                ship_weight(index)
            for k in range(K):
                red_c[s, k : k + 1] = jnp.sum(tacc[k], axis=0, keepdims=True)
            spread_from(red_c, 2)

        @pl.when(i == NCH)
        def _():
            gtaps[...] = collect(red_c, 2)[0:K]

            for index, out in ((2, gwo), (0, gwv), (1, gwg)):
                slots = wrecv.at[index, pl.ds(0, NS - 1)]
                pltpu.make_async_copy(slots, slots, wr_recv.at[index]).wait()
                total = wrecv[index, 0].astype(F32)
                for k in range(1, NS):
                    total = total + wrecv[index, k].astype(F32)
                out[...] = total

        @pl.when(jnp.logical_and(i >= LAG_B, i < NCH + LAG_B))
        def _():
            far_sends(*turn_of(i - LAG_B))

        @pl.when(i >= LAG_C)
        def _():
            finish(*turn_of(i - LAG_C))

        return carry

    lax.fori_loop(0, NCH + LAG_C, homeward, 0)

    for copy in next_weights:
        copy.wait_send()
    weight_swap.wait_send()
    for kind in range(2):
        for copy in edge_copies(kind):
            copy.wait_send()
    red_sent(red_a, 0)
    red_sent(red_b, 1)
    red_sent(red_c, 2)
    for index in range(3):
        slots = wrecv.at[index, pl.ds(0, NS - 1)]
        pltpu.make_async_copy(slots, slots, wr_send.at[index]).wait()

    def sent(whole, semaphore):
        pltpu.make_async_copy(whole, whole, semaphore).wait()

    sent(gmine, ge_send)
    sent(gg_out, gg_send)
    sent(far_out, fr_send)
    for q in range(NCH):
        own_copy(q).wait()
    others = osend.at[:, pl.ds(0, NS - 1)]
    sent(others, aa_send)
    sent(others, aa_recv)


def hand_on(*refs):
    half = (len(refs) - 1) // 2
    sems = refs[-1]
    copies = [pltpu.make_async_copy(refs[i], refs[half + i], sems.at[i]) for i in range(half)]
    for copy in copies:
        copy.start()
    for copy in copies:
        copy.wait()


def per_device(
    normed,
    grad_out,
    value_weight,
    gate_weight,
    depth_taps,
    norm_gain,
    norm_shift,
    out_weight,
    lengths,
):
    R, NF, D = normed.shape
    K, CW = depth_taps.shape
    NS = lax.axis_size("seq")
    M = 8 * NS
    F = min(512, NF)
    TM = min(1024, NF)
    TC = min(128, F)
    NCH = R * NF // F
    DP = D // NS
    cfg = (R, NF, D, NS, F, TM, TC)
    vmem = pl.BlockSpec(memory_space=pltpu.VMEM)
    hbm = pl.BlockSpec(memory_space=pl.ANY)
    dma = pltpu.SemaphoreType.DMA
    padded = NF + 2 * PAD
    out_shape = (
        jax.ShapeDtypeStruct((R, 8, NS * NF), BF16),
        jax.ShapeDtypeStruct((DP, CW), F32),
        jax.ShapeDtypeStruct((DP, CW), F32),
        jax.ShapeDtypeStruct((DP, CW), F32),
        jax.ShapeDtypeStruct((K, CW), F32),
        jax.ShapeDtypeStruct((1, CW), F32),
        jax.ShapeDtypeStruct((1, CW), F32),
    )
    scratch = [
        pltpu.VMEM((R, NF, D), BF16),
        pltpu.VMEM((R, NF, D), BF16),
        pltpu.VMEM((D, 2 * LANES), BF16),
        pltpu.VMEM((D, 2 * LANES), BF16),
        pltpu.VMEM((2, D, 2 * LANES), BF16),
        pltpu.VMEM((2, 2, 2 * M, 2 * LANES), BF16),
        pltpu.VMEM((2, 2, 2 * M, 2 * LANES), BF16),
        pltpu.VMEM((2, 2, 2 * M, 2 * LANES), BF16),
        pltpu.VMEM((R, NF, LANES), BF16),
        pltpu.VMEM((NCH, M, F), F32),
        pltpu.VMEM((R, padded, LANES), F32),
        pltpu.VMEM((R, NF, LANES), F32),
        pltpu.VMEM((R, NF, LANES), F32),
        pltpu.VMEM((R, padded, LANES), F32),
        pltpu.VMEM((R, padded, LANES), F32),
        pltpu.VMEM((R, padded, LANES), F32),
        pltpu.VMEM((R, NF, LANES), BF16),
        pltpu.VMEM((2, 2, R, EDGE, LANES), F32),
        pltpu.VMEM((2, 2, R, EDGE, LANES), F32),
        pltpu.VMEM((NS, 8, LANES), F32),
        pltpu.VMEM((NS, 8, LANES), F32),
        pltpu.VMEM((NS, 16, LANES), F32),
        pltpu.VMEM((NCH, F, LANES), BF16),
        pltpu.VMEM((NCH, F, LANES), BF16),
        pltpu.VMEM((NCH, 2, F, 2 * LANES), BF16),
        pltpu.VMEM((NCH, 2, F, 2 * LANES), BF16),
        pltpu.VMEM((NCH, M, F), BF16),
        pltpu.VMEM((NCH, M, F), BF16),
        pltpu.VMEM((NCH, NS, 8, F), BF16),
        pltpu.VMEM((K, 8, LANES), F32),
        pltpu.VMEM((2 * LANES, D), F32),
        pltpu.VMEM((LANES, D), F32),
        pltpu.VMEM((3, D, LANES), BF16),
        pltpu.VMEM((3, NS, DP, LANES), BF16),
        dma((3 + 2 * R,)),
        dma((4,)),
        dma((4,)),
        dma((3,)),
        dma((3,)),
        dma,
        dma,
        dma((2,)),
        dma((2,)),
        dma,
        dma((2 * NCH,)),
        dma,
        dma((NCH,)),
        dma,
        dma((NCH,)),
        dma,
        dma,
        dma((NCH,)),
        dma((3,)),
        dma((3,)),
    ]
    outs = pl.pallas_call(
        functools.partial(kernel, cfg),
        out_shape=tuple(pltpu.VMEM(o.shape, o.dtype) for o in out_shape),
        in_specs=[pl.BlockSpec(memory_space=pltpu.SMEM)] + [hbm] * 5 + [vmem] * 3,
        out_specs=(vmem,) * 7,
        scratch_shapes=scratch,
        compiler_params=pltpu.CompilerParams(
            collective_id=0, has_side_effects=True, vmem_limit_bytes=60 * 1024 * 1024
        ),
        cost_estimate=pl.CostEstimate(
            flops=8 * 2 * R * NF * D * CW, bytes_accessed=4 * R * NF * D, transcendentals=0
        ),
    )(
        lengths,
        normed,
        grad_out,
        value_weight,
        gate_weight,
        out_weight,
        depth_taps,
        norm_gain.reshape(1, CW),
        norm_shift.reshape(1, CW),
    )
    held = [pltpu.with_memory_space_constraint(o, pltpu.VMEM) for o in outs]
    moved = pl.pallas_call(
        hand_on,
        out_shape=out_shape,
        in_specs=[vmem] * len(out_shape),
        out_specs=(hbm,) * len(out_shape),
        scratch_shapes=[dma((len(out_shape),))],
    )(*held)
    grad_in, grad_wv, grad_wg, grad_wo, grad_taps, grad_gain, grad_shift = moved
    return (
        grad_in,
        grad_wv,
        grad_wg,
        grad_wo,
        grad_taps,
        grad_gain.reshape(CW),
        grad_shift.reshape(CW),
    )


def solution(mesh):
    placed = (
        P(None, "seq", None),
        P(None, "seq", None),
        P(None, "tp"),
        P(None, "tp"),
        P(None, "tp"),
        P("tp"),
        P("tp"),
        P(None, "tp"),
        P(),
    )
    return jax.shard_map(
        per_device,
        mesh=mesh,
        in_specs=placed,
        out_specs=(
            P(None, ("seq", "tp"), None),
            P("seq", "tp"),
            P("seq", "tp"),
            P("seq", "tp"),
            P(None, "tp"),
            P("tp"),
            P("tp"),
        ),
        check_vma=False,
    )
```

```python
import functools

import jax
import jax.numpy as jnp
from jax import lax
from jax.experimental import pallas as pl
from jax.experimental.pallas import tpu as pltpu
from jax.sharding import PartitionSpec as P

MESH = pl.DeviceIdType.MESH
F32 = jnp.float32
BF16 = jnp.bfloat16
EPS = 1e-05
LANES = 128
EDGE = 8
PAD = 16
XN = 4


def mm(a, b):
    return jnp.dot(a, b, preferred_element_type=F32)


def mm_t(a, b):
    return lax.dot_general(a, b, (((1,), (1,)), ((), ())), preferred_element_type=F32)


def mm_tl(a, b):
    return lax.dot_general(a, b, (((0,), (0,)), ((), ())), preferred_element_type=F32)


def fold(v):
    rows = v.shape[0]
    return jnp.sum(v.reshape(rows // 8, 8, LANES), axis=0)


def kernel(
    cfg,
    lengths,
    normed_h,
    grads_h,
    wv_h,
    wg_h,
    wo_h,
    taps,
    gain,
    shift,
    gin,
    gwv,
    gwg,
    gwo,
    gtaps,
    ggain,
    gshift,
    nv,
    gv,
    wcat,
    wo,
    w_next,
    wd,
    wd_send,
    wd_oth,
    feats,
    own_part,
    gp,
    gs,
    a2,
    cv,
    gn,
    gc,
    sw,
    halo_out,
    halo,
    red_a,
    red_b,
    red_c,
    gg_out,
    gg_in,
    gmine,
    gother,
    far_out,
    far_in,
    osend,
    tacc,
    wacc,
    woacc,
    wsend,
    wrecv,
    load_sem,
    halo_send,
    halo_recv,
    red_send,
    red_recv,
    wx_send,
    wx_recv,
    wn_send,
    wn_recv,
    ge_send,
    ge_recv,
    gg_send,
    gg_recv,
    fr_send,
    fr_recv,
    aa_send,
    aa_recv,
    aa_own,
    wr_send,
    wr_recv,
):
    R, NF, D, NS, F, TM, TC = cfg
    K = taps.shape[0]
    H = (K - 1) // 2
    M = 8 * NS
    NCH = R * NF // F
    cpr = NF // F
    DP = D // NS
    s = lax.axis_index("seq")
    t = lax.axis_index("tp")
    x = lax.div(t, 2)
    core = lax.rem(t, 2)
    other = x * 2 + (1 - core)
    step = 1 - 2 * lax.rem(x, 2)
    x_pair = (x + step, lax.rem(x + XN - step, XN))
    pair = tuple(xp * 2 + core for xp in x_pair)
    up = lax.rem(s + 1, NS)
    down = lax.rem(s + NS - 1, NS)

    barrier = pltpu.get_barrier_semaphore()

    def greet(k, carry):
        pl.semaphore_signal(
            barrier, inc=1, device_id=(lax.rem(s + k, NS), t), device_id_type=MESH
        )
        return carry

    lax.fori_loop(1, NS, greet, 0)
    for mate in (other,) + pair:
        pl.semaphore_signal(barrier, inc=1, device_id=(s, mate), device_id_type=MESH)

    loads = [
        pltpu.make_async_copy(wv_h, wcat.at[:, 0:LANES], load_sem.at[0]),
        pltpu.make_async_copy(wg_h, wcat.at[:, LANES : 2 * LANES], load_sem.at[1]),
        pltpu.make_async_copy(wo_h, wo.at[:, 0:LANES], load_sem.at[2]),
    ]
    for load in loads:
        load.start()

    def normed_load(r):
        return pltpu.make_async_copy(normed_h.at[r], nv.at[r], load_sem.at[3 + r])

    def grads_load(r):
        return pltpu.make_async_copy(grads_h.at[r], gv.at[r], load_sem.at[3 + R + r])

    for r in range(R):
        normed_load(r).start()

    def valid(r, row0, rows):
        at = s * NF + row0 + lax.broadcasted_iota(jnp.int32, (rows, LANES), 0)
        return jnp.logical_and(at >= 0, at < lengths[r])

    def picker(xd, cd):
        row = lax.broadcasted_iota(jnp.int32, (M, D), 0)
        col = lax.broadcasted_iota(jnp.int32, (M, D), 1)
        want = (row // 8) * 64 + xd * 16 + cd * 8 + row % 8
        return jnp.where(col == want, 1.0, 0.0).astype(BF16)

    feature = lax.broadcasted_iota(jnp.int32, (D, LANES), 0)
    place = lax.broadcasted_iota(jnp.int32, (D, LANES), 1)
    want = (place // 8) * 64 + x * 16 + core * 8 + place % 8
    wo[:, LANES : 2 * LANES] = jnp.where(
        jnp.logical_and(feature == want, place < M), 1.0, 0.0
    ).astype(BF16)
    loads[0].wait()
    loads[1].wait()

    def pick_weights(first):
        for cd, out in ((core, wd), (1 - core, wd_send)):
            pick = picker(x, cd)
            if first:
                own = mm(pick, wcat[...]).astype(BF16)
            for half in range(2):
                if first:
                    out[half, 0, 0:M] = own
                else:
                    out[half, 1, 0:M] = mm(pick, w_next[half]).astype(BF16)
            for half in range(2):
                pick = picker(x_pair[1 - half], cd)
                source = wcat[...] if first else w_next[half]
                out[half, 0 if first else 1, M : 2 * M] = mm(pick, source).astype(BF16)

    tacc[...] = jnp.zeros_like(tacc)
    wacc[...] = jnp.zeros_like(wacc)
    woacc[...] = jnp.zeros_like(woacc)
    for r in range(R):
        gp[r, 0 : PAD - EDGE] = jnp.zeros((PAD - EDGE, LANES), F32)
        gp[r, NF + PAD + EDGE : NF + 2 * PAD] = jnp.zeros((PAD - EDGE, LANES), F32)

    def remote(src, dst, send, recv, device):
        return pltpu.make_async_remote_copy(
            src_ref=src,
            dst_ref=dst,
            send_sem=send,
            recv_sem=recv,
            device_id=device,
            device_id_type=MESH,
        )

    def edge_copies(kind):
        return (
            remote(
                halo_out.at[kind, 0],
                halo.at[kind, 0],
                halo_send.at[2 * kind],
                halo_recv.at[2 * kind],
                (up, t),
            ),
            remote(
                halo_out.at[kind, 1],
                halo.at[kind, 1],
                halo_send.at[2 * kind + 1],
                halo_recv.at[2 * kind + 1],
                (down, t),
            ),
        )

    def send_edges(kind, field):
        for r in range(R):
            halo_out[kind, 0, r] = field[r, PAD + NF - EDGE : PAD + NF]
            halo_out[kind, 1, r] = field[r, PAD : PAD + EDGE]
        for copy in edge_copies(kind):
            copy.start()

    def take_edges(kind, field):
        for copy in edge_copies(kind):
            copy.wait_recv()
        for r in range(R):
            field[r, PAD - EDGE : PAD] = jnp.where(s > 0, halo[kind, 0, r], 0.0)
            field[r, PAD + NF : PAD + NF + EDGE] = jnp.where(s < NS - 1, halo[kind, 1, r], 0.0)

    per_rec = NF // TM

    def forward(i, carry):
        r = lax.div(i, per_rec)
        part = lax.rem(i, per_rec)
        row0 = pl.multiple_of(part * TM, TM)
        rows = pl.ds(row0, TM)

        @pl.when(part == 0)
        def _():
            normed_load(r).wait()
            grads_load(r).start()

        both = mm(nv[r, rows, :], wcat[...])
        gate = jax.nn.sigmoid(both[:, LANES:])
        unit = both[:, :LANES] * gate
        gp[r, pl.ds(row0 + PAD, TM)] = jnp.where(valid(r, row0, TM), unit, 0.0)
        gs[r, rows] = gate
        a2[r, rows] = unit * (1.0 - gate)
        return carry

    lax.fori_loop(0, R * per_rec, forward, 0)
    pl.semaphore_wait(barrier, NS - 1 + 3)
    send_edges(0, gp)
    next_weights = [
        remote(wcat, w_next.at[half], wn_send.at[half], wn_recv.at[half], (s, pair[half]))
        for half in range(2)
    ]
    for copy in next_weights:
        copy.start()
    weight_swap = remote(wd_send, wd_oth, wx_send, wx_recv, (s, other))

    tap_rows = [taps[k : k + 1, :] for k in range(K)]
    tiles = NF // TC
    zero = jnp.zeros((8, LANES), F32)

    def conv_at(r, start, rows):
        total = tap_rows[0] * gp[r, pl.ds(start + PAD - H, rows)]
        for k in range(1, K):
            total = total + tap_rows[k] * gp[r, pl.ds(start + PAD - H + k, rows)]
        return total

    def conv_tile(r, i, sums):
        row0 = pl.multiple_of(i * TC, TC)
        total = conv_at(r, row0, TC)
        cv[r, pl.ds(row0 + PAD, TC)] = total
        kept = jnp.where(valid(r, row0, TC), total, 0.0)
        return sums[0] + fold(kept), sums[1] + fold(kept * kept)

    def conv_inner(r, sums):
        return lax.fori_loop(1, tiles - 1, functools.partial(conv_tile, r), sums)

    sums = lax.fori_loop(0, R, conv_inner, (zero, zero))
    loads[2].wait()

    def back_one(i, carry):
        r = lax.div(i, per_rec)
        part = lax.rem(i, per_rec)
        row0 = pl.multiple_of(part * TM, TM)

        @pl.when(part == 0)
        def _():
            grads_load(r).wait()

        both = mm(gv[r, pl.ds(row0, TM), :], wo[...])
        gn[r, pl.ds(row0 + PAD, TM)] = both[:, :LANES]
        feats[r, pl.ds(row0, TM)] = both[:, LANES:].astype(BF16)
        return carry

    lax.fori_loop(0, per_rec, back_one, 0)
    take_edges(0, gp)

    def conv_outer(r, sums):
        sums = conv_tile(r, 0, sums)
        return conv_tile(r, tiles - 1, sums)

    sums = lax.fori_loop(0, R, conv_outer, sums)

    def red_wait(red, index):
        part = red.at[pl.ds(0, NS - 1)]
        pltpu.make_async_copy(part, part, red_recv.at[index]).wait()

    def red_sent(red, index):
        part = red.at[pl.ds(0, NS - 1)]
        pltpu.make_async_copy(part, part, red_send.at[index]).wait()

    def spread_from(red, index):
        def give(k, carry):
            remote(
                red.at[s], red.at[s], red_send.at[index], red_recv.at[index], (lax.rem(s + k, NS), t)
            ).start()
            return carry

        lax.fori_loop(1, NS, give, 0)

    def spread(red, index, value):
        red[s] = value
        spread_from(red, index)

    def two_rows(first, second):
        row = lax.broadcasted_iota(jnp.int32, (8, LANES), 0)
        first = jnp.sum(first, axis=0, keepdims=True)
        second = jnp.sum(second, axis=0, keepdims=True)
        return jnp.where(row == 0, first, jnp.where(row == 1, second, 0.0))

    def collect(red, index):
        red_wait(red, index)
        total = red[0]
        for k in range(1, NS):
            total = total + red[k]
        return total

    spread(red_a, 0, two_rows(*sums))

    for r in range(R):
        cv[r, PAD - EDGE : PAD] = conv_at(r, -EDGE, EDGE)
        cv[r, PAD + NF : PAD + NF + EDGE] = conv_at(r, NF, EDGE)
    def chunk_place(q):
        r = lax.div(q, cpr)
        return r, pl.multiple_of(lax.rem(q, cpr) * F, F)

    lax.fori_loop(per_rec, R * per_rec, back_one, 0)
    pick_weights(True)

    total = collect(red_a, 0)
    count = (lengths[0] + lengths[1] + lengths[2] + lengths[3]).astype(F32)
    inv_count = 1.0 / jnp.full((1, LANES), count, F32)
    centre = total[0:1] * inv_count
    spread_sq = total[1:2] * inv_count - centre * centre
    inv_std = lax.rsqrt(spread_sq + EPS)
    gain_row = gain[...]
    shift_row = shift[...]

    def norm_rec(r, sums):
        def norm_tile(i, sums):
            row0 = pl.multiple_of(i * TC, TC)
            rows = pl.ds(row0, TC)
            padded = pl.ds(row0 + PAD, TC)
            unit = (cv[r, padded] - centre) * inv_std
            normalized = unit * gain_row + shift_row
            sig = jax.nn.sigmoid(normalized)
            ok = valid(r, row0, TC)
            sw[r, rows] = jnp.where(ok, normalized * sig, 0.0).astype(BF16)
            grad = gn[r, padded] * sig * (1.0 + normalized * (1.0 - sig))
            grad = jnp.where(ok, grad, 0.0)
            gn[r, padded] = grad
            return sums[0] + fold(grad), sums[1] + fold(grad * unit)

        return lax.fori_loop(0, tiles, norm_tile, sums)

    sums = lax.fori_loop(0, R, norm_rec, (zero, zero))
    spread(red_b, 1, two_rows(*sums))
    send_edges(1, gn)

    def out_weight_part(q, carry):
        r, row0 = chunk_place(q)
        rows = pl.ds(row0, F)
        woacc[...] += mm_tl(sw[r, rows, :], gv[r, rows, :])
        return carry

    lax.fori_loop(0, NCH, out_weight_part, 0)

    def turn_weight(index, acc, first):
        for b in range(D // LANES):
            wsend[index, b * LANES : (b + 1) * LANES, :] = jnp.transpose(
                acc[first : first + LANES, b * LANES : (b + 1) * LANES]
            ).astype(BF16)

    def ship_weight(index):
        def give(k, carry):
            p = lax.rem(s + k, NS)
            remote(
                wsend.at[index, pl.ds(pl.multiple_of(p * DP, DP), DP)],
                wrecv.at[index, s],
                wr_send.at[index],
                wr_recv.at[index],
                (p, t),
            ).start()
            return carry

        lax.fori_loop(1, NS, give, 0)
        wrecv[index, s] = wsend[index, pl.ds(pl.multiple_of(s * DP, DP), DP)]

    turn_weight(2, woacc, 0)
    for copy in next_weights:
        copy.wait_recv()
    pick_weights(False)
    weight_swap.start()
    total = collect(red_b, 1)
    ship_weight(2)
    gshift[...] = total[0:1]
    ggain[...] = total[1:2]
    scale = gain_row * inv_std
    mean_shift = total[0:1] * inv_count
    mean_gain = total[1:2] * inv_count

    take_edges(1, gn)
    padded_rows = NF + 2 * EDGE
    TE = padded_rows // 10 if padded_rows % 80 == 0 else 8

    def conv_grad(r):
        def conv_grad_tile(i, carry):
            row0 = pl.multiple_of(i * TE, TE)
            rows = pl.ds(row0 + PAD - EDGE, TE)
            unit = (cv[r, rows] - centre) * inv_std
            grad = scale * (gn[r, rows] - mean_shift - unit * mean_gain)
            gc[r, rows] = jnp.where(valid(r, row0 - EDGE, TE), grad, 0.0)
            return carry

        lax.fori_loop(0, padded_rows // TE, conv_grad_tile, 0)

    def swap_copy(q, group):
        return remote(
            gmine.at[q, group],
            gother.at[q, group],
            ge_send,
            ge_recv.at[2 * q + group],
            (s, other),
        )

    def turn_of(i):
        half = lax.rem(i, 2)
        return half, half * (NCH // 2) + lax.div(i, 2)

    def pair_copy(half, q):
        to = pair[0] * (1 - half) + pair[1] * half
        return remote(gg_out.at[q], gg_in.at[q], gg_send, gg_recv.at[q], (s, to))

    def far_copy(half, q):
        to = pair[1] * (1 - half) + pair[0] * half
        return remote(far_out.at[q], far_in.at[q], fr_send, fr_recv.at[q], (s, to))

    def pointwise_grads(q):
        r, base = chunk_place(q)

        def tile(i, taps_sum):
            row0 = pl.multiple_of(base + i * TC, TC)
            rows = pl.ds(row0, TC)
            here = pl.ds(pl.multiple_of(i * TC, TC), TC)
            grad = tap_rows[0] * gc[r, pl.ds(row0 + PAD + H, TC)]
            for k in range(1, K):
                grad = grad + tap_rows[k] * gc[r, pl.ds(row0 + PAD + H - k, TC)]
            grad = jnp.where(valid(r, row0, TC), grad, 0.0)
            gg_out[q, here] = grad.astype(BF16)
            gmine[q, 0, here, 0:LANES] = (grad * gs[r, rows]).astype(BF16)
            gmine[q, 0, here, LANES : 2 * LANES] = (grad * a2[r, rows]).astype(BF16)
            centre_rows = gc[r, pl.ds(row0 + PAD, TC)]
            return tuple(
                taps_sum[k] + fold(centre_rows * gp[r, pl.ds(row0 + PAD - H + k, TC)])
                for k in range(K)
            )

        taps_sum = lax.fori_loop(0, F // TC, tile, tuple(tacc[k] for k in range(K)))
        for k in range(K):
            tacc[k] = taps_sum[k]

    def pair_grads(half, q):
        r, row0 = chunk_place(q)
        both = mm(nv[r, pl.ds(row0, F), :], w_next[half])
        gate = jax.nn.sigmoid(both[:, LANES:])
        unit = both[:, :LANES] * gate
        pair_copy(half, q).wait_recv()
        grad = gg_in[q].astype(F32)
        gmine[q, 1, :, 0:LANES] = (grad * gate).astype(BF16)
        gmine[q, 1, :, LANES : 2 * LANES] = (grad * (unit * (1.0 - gate))).astype(BF16)
        swap_copy(q, 1).start()

    row = lax.broadcasted_iota(jnp.int32, (M, LANES), 0)
    col = lax.broadcasted_iota(jnp.int32, (M, LANES), 1)
    own_rows = jnp.where(row == col, 1.0, 0.0).astype(BF16)

    def far_sends(half, q):
        r, row0 = chunk_place(q)
        total = mm_t(wd[half, 0], gmine[q, 0]) + mm_t(wd[half, 1], gmine[q, 1])
        for group in range(2):
            swap_copy(q, group).wait_recv()
        total = total + (mm_t(wd_oth[half, 0], gother[q, 0]) + mm_t(wd_oth[half, 1], gother[q, 1]))
        far_out[q] = total[M:].astype(BF16)
        far_copy(half, q).start()
        own_part[q] = total[:M] + mm_t(own_rows, feats[r, pl.ds(row0, F)])

    def out_place(q, owner):
        r, row0 = chunk_place(q)
        return gin.at[r, :, pl.ds(pl.multiple_of(owner * NF + row0, F), F)]

    def own_copy(q):
        return pltpu.make_async_copy(osend.at[q, s], out_place(q, s), aa_own.at[q])

    def finish(half, q):
        far_copy(half, q).wait_recv()
        total = own_part[q] + far_in[q].astype(F32)
        osend[q] = total.astype(BF16).reshape(NS, 8, F)

        def give(k, carry):
            p = lax.rem(s + k, NS)
            remote(osend.at[q, p], out_place(q, s), aa_send, aa_recv, (p, t)).start()
            return carry

        lax.fori_loop(1, NS, give, 0)
        own_copy(q).start()

    def weight_part(q):
        r, row0 = chunk_place(q)
        wacc[...] += mm_tl(gmine[q, 0], nv[r, pl.ds(row0, F), :])

    for k in range(K, 16):
        red_c[s, k : k + 1] = jnp.zeros((1, LANES), F32)

    def outward(i, carry):
        half, q = turn_of(i)

        @pl.when(lax.rem(q, cpr) == 0)
        def _():
            conv_grad(lax.div(q, cpr))

        pointwise_grads(q)
        pair_copy(half, q).start()
        swap_copy(q, 0).start()

        @pl.when(i < NCH - 8)
        def _():
            weight_part(q)

        return carry

    lax.fori_loop(0, NCH, outward, 0)
    weight_swap.wait_recv()
    LAG_B, LAG_C = 1, 5

    def homeward(i, carry):
        @pl.when(i < NCH)
        def _():
            pair_grads(*turn_of(i))

        @pl.when(i < 2)
        def _():
            for k in range(4):
                weight_part(turn_of(NCH - 8 + 4 * i + k)[1])

        @pl.when(i == 1)
        def _():
            for index in range(2):
                turn_weight(index, wacc, index * LANES)
                ship_weight(index)
            for k in range(K):
                red_c[s, k : k + 1] = jnp.sum(tacc[k], axis=0, keepdims=True)
            spread_from(red_c, 2)

        @pl.when(i == NCH)
        def _():
            gtaps[...] = collect(red_c, 2)[0:K]

            for index, out in ((2, gwo), (0, gwv), (1, gwg)):
                slots = wrecv.at[index, pl.ds(0, NS - 1)]
                pltpu.make_async_copy(slots, slots, wr_recv.at[index]).wait()
                total = wrecv[index, 0].astype(F32)
                for k in range(1, NS):
                    total = total + wrecv[index, k].astype(F32)
                out[...] = total

        @pl.when(jnp.logical_and(i >= LAG_B, i < NCH + LAG_B))
        def _():
            far_sends(*turn_of(i - LAG_B))

        @pl.when(i >= LAG_C)
        def _():
            finish(*turn_of(i - LAG_C))

        return carry

    lax.fori_loop(0, NCH + LAG_C, homeward, 0)

    for copy in next_weights:
        copy.wait_send()
    weight_swap.wait_send()
    for kind in range(2):
        for copy in edge_copies(kind):
            copy.wait_send()
    red_sent(red_a, 0)
    red_sent(red_b, 1)
    red_sent(red_c, 2)
    for index in range(3):
        slots = wrecv.at[index, pl.ds(0, NS - 1)]
        pltpu.make_async_copy(slots, slots, wr_send.at[index]).wait()

    def sent(whole, semaphore):
        pltpu.make_async_copy(whole, whole, semaphore).wait()

    sent(gmine, ge_send)
    sent(gg_out, gg_send)
    sent(far_out, fr_send)
    for q in range(NCH):
        own_copy(q).wait()
    others = osend.at[:, pl.ds(0, NS - 1)]
    sent(others, aa_send)
    sent(others, aa_recv)


def hand_on(*refs):
    half = (len(refs) - 1) // 2
    sems = refs[-1]
    copies = [pltpu.make_async_copy(refs[i], refs[half + i], sems.at[i]) for i in range(half)]
    for copy in copies:
        copy.start()
    for copy in copies:
        copy.wait()


def per_device(
    normed,
    grad_out,
    value_weight,
    gate_weight,
    depth_taps,
    norm_gain,
    norm_shift,
    out_weight,
    lengths,
):
    R, NF, D = normed.shape
    K, CW = depth_taps.shape
    NS = lax.axis_size("seq")
    M = 8 * NS
    F = min(512, NF)
    TM = min(1024, NF)
    TC = min(128, F)
    NCH = R * NF // F
    DP = D // NS
    cfg = (R, NF, D, NS, F, TM, TC)
    vmem = pl.BlockSpec(memory_space=pltpu.VMEM)
    hbm = pl.BlockSpec(memory_space=pl.ANY)
    dma = pltpu.SemaphoreType.DMA
    padded = NF + 2 * PAD
    out_shape = (
        jax.ShapeDtypeStruct((R, 8, NS * NF), BF16),
        jax.ShapeDtypeStruct((DP, CW), F32),
        jax.ShapeDtypeStruct((DP, CW), F32),
        jax.ShapeDtypeStruct((DP, CW), F32),
        jax.ShapeDtypeStruct((K, CW), F32),
        jax.ShapeDtypeStruct((1, CW), F32),
        jax.ShapeDtypeStruct((1, CW), F32),
    )
    scratch = [
        pltpu.VMEM((R, NF, D), BF16),
        pltpu.VMEM((R, NF, D), BF16),
        pltpu.VMEM((D, 2 * LANES), BF16),
        pltpu.VMEM((D, 2 * LANES), BF16),
        pltpu.VMEM((2, D, 2 * LANES), BF16),
        pltpu.VMEM((2, 2, 2 * M, 2 * LANES), BF16),
        pltpu.VMEM((2, 2, 2 * M, 2 * LANES), BF16),
        pltpu.VMEM((2, 2, 2 * M, 2 * LANES), BF16),
        pltpu.VMEM((R, NF, LANES), BF16),
        pltpu.VMEM((NCH, M, F), F32),
        pltpu.VMEM((R, padded, LANES), F32),
        pltpu.VMEM((R, NF, LANES), F32),
        pltpu.VMEM((R, NF, LANES), F32),
        pltpu.VMEM((R, padded, LANES), F32),
        pltpu.VMEM((R, padded, LANES), F32),
        pltpu.VMEM((R, padded, LANES), F32),
        pltpu.VMEM((R, NF, LANES), BF16),
        pltpu.VMEM((2, 2, R, EDGE, LANES), F32),
        pltpu.VMEM((2, 2, R, EDGE, LANES), F32),
        pltpu.VMEM((NS, 8, LANES), F32),
        pltpu.VMEM((NS, 8, LANES), F32),
        pltpu.VMEM((NS, 16, LANES), F32),
        pltpu.VMEM((NCH, F, LANES), BF16),
        pltpu.VMEM((NCH, F, LANES), BF16),
        pltpu.VMEM((NCH, 2, F, 2 * LANES), BF16),
        pltpu.VMEM((NCH, 2, F, 2 * LANES), BF16),
        pltpu.VMEM((NCH, M, F), BF16),
        pltpu.VMEM((NCH, M, F), BF16),
        pltpu.VMEM((NCH, NS, 8, F), BF16),
        pltpu.VMEM((K, 8, LANES), F32),
        pltpu.VMEM((2 * LANES, D), F32),
        pltpu.VMEM((LANES, D), F32),
        pltpu.VMEM((3, D, LANES), BF16),
        pltpu.VMEM((3, NS, DP, LANES), BF16),
        dma((3 + 2 * R,)),
        dma((4,)),
        dma((4,)),
        dma((3,)),
        dma((3,)),
        dma,
        dma,
        dma((2,)),
        dma((2,)),
        dma,
        dma((2 * NCH,)),
        dma,
        dma((NCH,)),
        dma,
        dma((NCH,)),
        dma,
        dma,
        dma((NCH,)),
        dma((3,)),
        dma((3,)),
    ]
    outs = pl.pallas_call(
        functools.partial(kernel, cfg),
        out_shape=tuple(pltpu.VMEM(o.shape, o.dtype) for o in out_shape),
        in_specs=[pl.BlockSpec(memory_space=pltpu.SMEM)] + [hbm] * 5 + [vmem] * 3,
        out_specs=(vmem,) * 7,
        scratch_shapes=scratch,
        compiler_params=pltpu.CompilerParams(
            collective_id=0, has_side_effects=True, vmem_limit_bytes=60 * 1024 * 1024
        ),
        cost_estimate=pl.CostEstimate(
            flops=8 * 2 * R * NF * D * CW, bytes_accessed=4 * R * NF * D, transcendentals=0
        ),
    )(
        lengths,
        normed,
        grad_out,
        value_weight,
        gate_weight,
        out_weight,
        depth_taps,
        norm_gain.reshape(1, CW),
        norm_shift.reshape(1, CW),
    )
    held = [pltpu.with_memory_space_constraint(o, pltpu.VMEM) for o in outs]
    moved = pl.pallas_call(
        hand_on,
        out_shape=out_shape,
        in_specs=[vmem] * len(out_shape),
        out_specs=(hbm,) * len(out_shape),
        scratch_shapes=[dma((len(out_shape),))],
    )(*held)
    grad_in, grad_wv, grad_wg, grad_wo, grad_taps, grad_gain, grad_shift = moved
    return (
        grad_in,
        grad_wv,
        grad_wg,
        grad_wo,
        grad_taps,
        grad_gain.reshape(CW),
        grad_shift.reshape(CW),
    )


def solution(mesh):
    placed = (
        P(None, "seq", None),
        P(None, "seq", None),
        P(None, "tp"),
        P(None, "tp"),
        P(None, "tp"),
        P("tp"),
        P("tp"),
        P(None, "tp"),
        P(),
    )
    return jax.shard_map(
        per_device,
        mesh=mesh,
        in_specs=placed,
        out_specs=(
            P(None, ("seq", "tp"), None),
            P("seq", "tp"),
            P("seq", "tp"),
            P("seq", "tp"),
            P(None, "tp"),
            P("tp"),
            P("tp"),
        ),
        check_vma=False,
    )
```
